32 devices in a mesh: dp: 4 (over y, core), blk: 2 (over x), mp: 4 (over z).
Axes of the slice: x: 2, y: 2, z: 4, core: 2. Of those that a mesh axis runs over, the one named last changes fastest.
Arguments:
- queries: bfloat16 [4, 320, 2048], P('dp', 'blk', 'mp'), may hold values from -16 to 16
- keys: bfloat16 [4, 320, 2048], P('dp', 'blk', 'mp'), may hold values from -16 to 16
- values: bfloat16 [4, 320, 2048], P('dp', 'blk', 'mp'), may hold values from -6 to 6
- clip_ids: int32 [4, 320], P('dp', 'blk'), may hold values from 0 to 1, never falling along the last dimension, each value on 1 to 240 neighbouring positions
- w_out: bfloat16 [2048, 4096], P('mp'), may hold values from -0.125 to 0.125
- cotangent: bfloat16 [4, 320, 4096], P('dp', 'blk', 'mp'), may hold values from -6 to 6
Outputs:
- mixed: bfloat16 [4, 320, 4096], P('dp', 'blk', 'mp')
- d_queries: bfloat16 [4, 320, 2048], P('dp', 'blk', 'mp')
- d_keys: bfloat16 [4, 320, 2048], P('dp', 'blk', 'mp')
- d_values: bfloat16 [4, 320, 2048], P('dp', 'blk', 'mp')
- d_w_out: float32 [2048, 4096], P('mp', ('dp', 'blk'))
The draws below stay inside these ranges and needn't reach their ends.
Inputs may be any that keep to these rules, and one draw needn't show every extreme that they name: `clip_ids`: each sequence holds clip 0 and then clip 1; each clip has at least 80 and at most 240 positions.
All inputs are finite; a program needn't handle non-finite values.
Results may differ from the reference program's by a relative error of at most 0.019.
Values may be sent and summed in bfloat16 or wider, within the bound.
A program may use at most 128 MiB of HBM per device.

```python
import math
import jax
import jax.numpy as jnp
import numpy as np
from jax import lax

D = 4096
H = 16
HD = 128
SEQ = 320
BATCH = 4
HC = 2048


def common_pair(key):
    base = jax.random.fold_in(key, 11)
    key_q, key_k = jax.random.split(base, 2)
    shape = (BATCH, SEQ, HC)
    q_val = jnp.clip(jax.random.normal(key_q, shape, jnp.float32), -4.0, 4.0)
    k_val = jnp.clip(jax.random.normal(key_k, shape, jnp.float32), -4.0, 4.0)
    return (q_val, k_val)


def draw_queries(key, part):
    return common_pair(key)[0].astype(jnp.bfloat16)


def draw_keys(key, part):
    return common_pair(key)[1].astype(jnp.bfloat16)


def shard_levels(own_key, shape, cuts, smallest, top_value):
    loudness, own = 1.0, jax.random.fold_in(own_key, 6)
    for dim, parts in cuts:
        draws = jnp.exp(jax.random.uniform(jax.random.fold_in(own, dim), (parts,), jnp.float32, smallest / len(cuts), top_value / len(cuts)))
        loudness = loudness * jnp.repeat(draws, shape[dim] // parts).reshape([-1 if axis == dim else 1 for axis in range(len(shape))])
    return loudness


def length_profile(amount, total, bound, skew):
    loads = [(1 << 20) // math.isqrt(standing ** skew) + 1 for standing in range(2, amount + 1)]
    spare, given = total - bound - (amount - 1), [1] * (amount - 1)
    while spare > 0:
        movable = [i for i in range(amount - 1) if given[i] < bound]
        whole, left = sum([loads[i] for i in movable]), spare
        for i in movable:
            extra = min(bound - given[i], max(1, left * loads[i] // whole), spare)
            given[i] = given[i] + extra
            spare = spare - extra
    return np.array([bound] + given)


def ragged(rng, count, total, bound, lean):
    if count == 2:
        one = jax.random.randint(rng, (), max(1, total - bound), min(bound, total - 1) + 1)
        return jnp.stack([one, total - one])
    tallies = jnp.asarray(length_profile(count, total, bound, lean), jnp.int32)
    twos = (count - 1) // 2
    source_of, sink = tallies[1:1 + 2 * twos:2], tallies[2:2 + 2 * twos:2]
    slack = jnp.minimum(source_of - 1, bound - sink)
    shifted = jax.random.randint(jax.random.fold_in(rng, 1), (twos,), 0, 1 << 20) % (slack + 1)
    tallies = tallies.at[1:1 + 2 * twos:2].set(source_of - shifted).at[2:2 + 2 * twos:2].set(sink + shifted)
    return tallies[jax.random.permutation(jax.random.fold_in(rng, 2), count)]


def centred(stream_key, extent, deviation, bound, cuts=(), kind=jnp.bfloat16):
    factor_of = shard_levels(stream_key, extent, cuts, -0.22, 0.18) if cuts else 1.0
    array = jax.random.normal(stream_key, extent, jnp.float32) * deviation * factor_of
    return jnp.minimum(jnp.maximum(array, -bound), bound).astype(kind)


def setup_inputs(seed: int = 0) -> dict:
    splits = jax.random.split(jax.random.key(seed), 7)
    return {
        "queries": draw_queries(jax.random.fold_in(splits[6], 71), 0),
        "keys": draw_keys(jax.random.fold_in(splits[6], 71), 0),
        "values": centred(splits[2], (BATCH, SEQ, HC), 1.0, 6.0, ((0, 4), (1, 2), (2, 4))),
        "clip_ids": jax.vmap(lambda own: jnp.searchsorted(jnp.cumsum(ragged(own, 2, SEQ, SEQ * 3 // 4, 0)), jnp.arange(SEQ), side="right"))(jax.random.split(splits[3], BATCH)).reshape((BATCH, SEQ)).astype(jnp.int32),
        "w_out": centred(splits[4], (HC, D), HC ** -0.5, 0.125, ((0, 4),)),
        "cotangent": centred(splits[5], (BATCH, SEQ, D), 1.0, 6.0, ((0, 4), (1, 2), (2, 4))),
    }


def one_sequence(items, w_out):
    q_in, k_in, v_in, clips, cot = items
    length = q_in.shape[0]
    scale = HD ** -0.5
    qh = q_in.reshape(length, H, HD).astype(jnp.float32)
    kh = k_in.reshape(length, H, HD).astype(jnp.float32)
    vh = v_in.reshape(length, H, HD).astype(jnp.float32)
    pos = jnp.arange(length, dtype=jnp.int32)
    seen = (pos[None, :] <= pos[:, None]) & (clips[None, :] == clips[:, None])
    scores = jnp.einsum('qhd,khd->hqk', qh, kh) * scale
    masked = jnp.where(seen[None], scores, -1e30)
    peak = jnp.max(masked, axis=-1)
    lse = peak + jnp.log(jnp.sum(jnp.where(seen[None], jnp.exp(masked - peak[:, :, None]), 0.0), axis=-1))
    probs = jnp.where(seen[None], jnp.exp(masked - lse[:, :, None]), 0.0)
    weights = probs.astype(jnp.bfloat16).astype(jnp.float32)
    attended = jnp.einsum('hqk,khd->qhd', probs, vh, precision=lax.Precision.HIGHEST).astype(jnp.bfloat16).reshape(length, H * HD)
    mixed = jnp.dot(attended, w_out, preferred_element_type=jnp.float32).astype(jnp.bfloat16)
    d_att = lax.dot_general(cot, w_out, (((1,), (1,)), ((), ())), preferred_element_type=jnp.float32).astype(jnp.bfloat16)
    doh = d_att.reshape(length, H, HD).astype(jnp.float32)
    delta = jnp.sum(doh * attended.reshape(length, H, HD).astype(jnp.float32), axis=-1)
    d_values = jnp.einsum('hqk,qhd->khd', weights, doh).astype(jnp.bfloat16).reshape(length, H * HD)
    d_probs = jnp.einsum('qhd,khd->hqk', doh, vh)
    d_scores = (probs * (d_probs - delta.T[:, :, None])).astype(jnp.bfloat16).astype(jnp.float32)
    d_queries = (jnp.einsum('hqk,khd->qhd', d_scores, kh) * scale).astype(jnp.bfloat16).reshape(length, H * HD)
    d_keys = (jnp.einsum('hqk,qhd->khd', d_scores, qh) * scale).astype(jnp.bfloat16).reshape(length, H * HD)
    d_w = lax.dot_general(attended, cot, (((0,), (0,)), ((), ())), preferred_element_type=jnp.float32)
    return mixed, d_queries, d_keys, d_values, d_w


def reference(queries, keys, values, clip_ids, w_out, cotangent):
    mixed, d_queries, d_keys, d_values, d_w = lax.map(lambda items: one_sequence(items, w_out), (queries, keys, values, clip_ids, cotangent))
    return mixed, d_queries, d_keys, d_values, jnp.sum(d_w, axis=0)
```

```python
import functools

import jax
import jax.numpy as jnp
from jax import lax
from jax.experimental import pallas as pl
from jax.experimental.pallas import tpu as pltpu
from jax.sharding import PartitionSpec as P

HD = 128
NEG = -1e30
MESH = pl.DeviceIdType.MESH
NN = (((1,), (0,)), ((), ()))
NT = (((1,), (1,)), ((), ()))
TN = (((0,), (0,)), ((), ()))


def dot(a, b, dims):
    return lax.dot_general(a, b, dims, preferred_element_type=jnp.float32)


def fused_kernel(
    nd, nm, chunks,
    q_ref, k_ref, v_ref, clip_ref, w_hbm, cot_ref,
    mixed_ref, dq_ref, dk_ref, dv_ref, dw_ref,
    w_ref, cot_full, cot_cols, att_all, kv_prev, clip_send, clip_prev,
    p_own, p_prev, d_att, dkv_own, dkv_send, dkv_recv,
    up_out, up_in, down_out, down_in,
    w_sem, own_sem, kv_ssem, kv_rsem, ag_up_ssem, ag_dn_ssem, ag_rsem,
    cc_ssem, cc_rsem, at_ssem, at_rsem,
    up_ssem, up_rsem, dn_ssem, dn_rsem, dkv_ssem, dkv_rsem,
):
    nb = 2
    d, b, m = lax.axis_index("dp"), lax.axis_index("blk"), lax.axis_index("mp")
    me = d * nb + b
    group = nd * nb
    rows, width = q_ref.shape[1], q_ref.shape[2]
    heads = width // HD
    scale = HD ** (-0.5)
    piece = cot_ref.shape[2]
    half = piece // nb
    part = piece // chunks

    def remote(src, dst, ssem, rsem, device):
        return pltpu.make_async_remote_copy(
            src_ref=src, dst_ref=dst, send_sem=ssem, recv_sem=rsem,
            device_id=device, device_id_type=MESH,
        )

    w_copy = pltpu.make_async_copy(w_hbm, w_ref, w_sem)
    w_copy.start()

    barrier = pltpu.get_barrier_semaphore()
    for off in range(1, group):
        other = lax.rem(me + off, group)
        pl.semaphore_signal(
            barrier, inc=1, device_id=(other // nb, lax.rem(other, nb), m), device_id_type=MESH
        )

    @pl.when(m > 0)
    def _():
        pl.semaphore_signal(barrier, inc=1, device_id=(d, b, m - 1), device_id_type=MESH)

    @pl.when(m < nm - 1)
    def _():
        pl.semaphore_signal(barrier, inc=1, device_id=(d, b, m + 1), device_id_type=MESH)

    clip_send[...] = jnp.zeros_like(clip_send)
    clip_send[0:1, 0:rows] = clip_ref[...]
    cot_full[m] = cot_ref[0]
    pl.semaphore_wait(
        barrier, group - 1 + jnp.where(m > 0, 1, 0) + jnp.where(m < nm - 1, 1, 0)
    )

    def kv_copies():
        peer = (d, 1, m)
        return (
            remote(k_ref.at[0], kv_prev.at[0], kv_ssem.at[0], kv_rsem.at[0], peer),
            remote(v_ref.at[0], kv_prev.at[1], kv_ssem.at[1], kv_rsem.at[1], peer),
            remote(clip_send, clip_prev, kv_ssem.at[2], kv_rsem.at[2], peer),
        )

    def gather_up(shard):
        return remote(
            cot_full.at[shard], cot_full.at[shard], ag_up_ssem.at[shard], ag_rsem.at[shard],
            (d, b, m + 1),
        )

    def gather_down(shard):
        return remote(
            cot_full.at[shard], cot_full.at[shard], ag_dn_ssem.at[shard], ag_rsem.at[shard],
            (d, b, m - 1),
        )

    def column_copy(shard, to_b):
        return remote(
            cot_full.at[shard, :, pl.ds(to_b * half, half)], cot_cols.at[me],
            cc_ssem.at[shard, to_b], cc_rsem.at[me], (shard, to_b, m),
        )

    def own_copy(to_b):
        return pltpu.make_async_copy(
            cot_full.at[d, :, pl.ds(to_b * half, half)], cot_cols.at[me], own_sem
        )

    def each_column(shard, away, here):
        for to_b in range(nb):
            is_me = jnp.logical_and(shard == d, b == to_b)

            @pl.when(jnp.logical_not(is_me))
            def _():
                away(column_copy(shard, to_b))

            @pl.when(is_me)
            def _():
                here(own_copy(to_b))

    def start(copy):
        copy.start()

    @pl.when(m < nm - 1)
    def _():
        gather_up(m).start()

    @pl.when(m > 0)
    def _():
        gather_down(m).start()

    @pl.when(b == 0)
    def _():
        for copy in kv_copies():
            copy.start()

    each_column(m, start, start)

    def gather_step(step):
        @pl.when(m - step >= 0)
        def _():
            shard = m - step
            gather_down(shard).wait_recv()

            @pl.when(m < nm - 1)
            def _():
                gather_up(shard).start()

            each_column(shard, start, start)

        @pl.when(m + step < nm)
        def _():
            shard = m + step
            gather_up(shard).wait_recv()

            @pl.when(m > 0)
            def _():
                gather_down(shard).start()

            each_column(shard, start, start)

    row = lax.broadcasted_iota(jnp.int32, (rows, rows), 0)
    col = lax.broadcasted_iota(jnp.int32, (rows, rows), 1)

    def clip_masks(use_prev):
        here = jnp.broadcast_to(clip_send[0:1, 0:rows], (rows, rows))
        mine = jnp.sum(jnp.where(row == col, here, 0), axis=1, keepdims=True)
        own = jnp.logical_and(col <= row, here == mine)
        prev = None
        if use_prev:
            prev = jnp.broadcast_to(clip_prev[0:1, 0:rows], (rows, rows)) == mine
        return own, prev

    def forward(use_prev):
        own, prev = clip_masks(use_prev)
        for h in range(heads):
            cols = pl.ds(h * HD, HD)
            q = q_ref[0, :, cols]
            s = jnp.where(own, dot(q, k_ref[0, :, cols], NT) * scale, NEG)
            peak = jnp.max(s, axis=1, keepdims=True)
            if use_prev:
                t = jnp.where(prev, dot(q, kv_prev[0, :, cols], NT) * scale, NEG)
                peak = jnp.maximum(peak, jnp.max(t, axis=1, keepdims=True))
            e = jnp.exp(s - peak)
            total = jnp.sum(e, axis=1, keepdims=True)
            if use_prev:
                f = jnp.exp(t - peak)
                total = total + jnp.sum(f, axis=1, keepdims=True)
            inverse = 1.0 / total
            e = e * inverse
            p_own[h] = e
            att = dot(e.astype(jnp.bfloat16), v_ref[0, :, cols], NN)
            if use_prev:
                f = f * inverse
                p_prev[h] = f
                att = att + dot(f.astype(jnp.bfloat16), kv_prev[1, :, cols], NN)
            att_all[me, :, cols] = att.astype(jnp.bfloat16)

    @pl.when(b == 0)
    def _():
        forward(False)

    gather_step(1)

    @pl.when(b == 1)
    def _():
        for copy in kv_copies():
            copy.wait_recv()
        forward(True)

    def att_copy(off):
        other = lax.rem(me + off, group)
        return remote(
            att_all.at[me], att_all.at[me], at_ssem.at[off], at_rsem.at[me],
            (other // nb, lax.rem(other, nb), m),
        )

    for off in range(1, group):
        att_copy(off).start()

    w_copy.wait()

    def partial(dest, c):
        at = pl.multiple_of(dest * piece + c * part, part)
        return dot(att_all[me], w_ref[:, pl.ds(at, part)], NN)

    def sum_up(dest, c):
        return remote(
            up_out.at[dest, c], up_in.at[dest, c], up_ssem.at[dest, c], up_rsem.at[dest, c],
            (d, b, m + 1),
        )

    def sum_down(dest, c):
        return remote(
            down_out.at[dest, c], down_in.at[dest, c], dn_ssem.at[dest, c], dn_rsem.at[dest, c],
            (d, b, m - 1),
        )

    def chain_step(step):
        for c in range(chunks):
            @pl.when(step >= m)
            def _():
                dest = nm - 1 - step + m
                mine = partial(dest, c)

                @pl.when(m == 0)
                def _():
                    up_out[dest, c] = mine.astype(jnp.bfloat16)

                @pl.when(m > 0)
                def _():
                    sum_up(dest, c).wait_recv()
                    up_out[dest, c] = (
                        mine + up_in[dest, c].astype(jnp.float32)
                    ).astype(jnp.bfloat16)

                sum_up(dest, c).start()

            @pl.when(step >= nm - 1 - m)
            def _():
                dest = step - (nm - 1 - m)
                mine = partial(dest, c)

                @pl.when(m == nm - 1)
                def _():
                    down_out[dest, c] = mine.astype(jnp.bfloat16)

                @pl.when(m < nm - 1)
                def _():
                    sum_down(dest, c).wait_recv()
                    down_out[dest, c] = (
                        mine + down_in[dest, c].astype(jnp.float32)
                    ).astype(jnp.bfloat16)

                sum_down(dest, c).start()

    for step in range(nm - 2):
        chain_step(step)
        gather_step(step + 2)

    total = dot(cot_full[0], w_ref[:, 0:piece], NT)
    for shard in range(1, nm):
        total = total + dot(cot_full[shard], w_ref[:, shard * piece:(shard + 1) * piece], NT)
    d_att[...] = total.astype(jnp.bfloat16)

    def dkv_copy():
        return remote(dkv_send, dkv_recv, dkv_ssem, dkv_rsem, (d, 0, m))

    def backward(use_prev):
        for h in range(heads):
            cols = pl.ds(h * HD, HD)
            do = d_att[:, cols]
            q = q_ref[0, :, cols]
            delta = jnp.sum(
                do.astype(jnp.float32) * att_all[me, :, cols].astype(jnp.float32),
                axis=1, keepdims=True,
            )
            e = p_own[h]
            ds = (e * (dot(do, v_ref[0, :, cols], NT) - delta)).astype(jnp.bfloat16)
            dq = dot(ds, k_ref[0, :, cols], NN)
            dk = dot(ds, q, TN) * scale
            dv = dot(e.astype(jnp.bfloat16), do, TN)
            if use_prev:
                f = p_prev[h]
                dt = (f * (dot(do, kv_prev[1, :, cols], NT) - delta)).astype(jnp.bfloat16)
                dq = dq + dot(dt, kv_prev[0, :, cols], NN)
                dkv_send[0, :, cols] = (dot(dt, q, TN) * scale).astype(jnp.bfloat16)
                dkv_send[1, :, cols] = dot(f.astype(jnp.bfloat16), do, TN).astype(jnp.bfloat16)
                dk_ref[0, :, cols] = dk.astype(jnp.bfloat16)
                dv_ref[0, :, cols] = dv.astype(jnp.bfloat16)
            else:
                dkv_own[0, :, cols] = dk
                dkv_own[1, :, cols] = dv
            dq_ref[0, :, cols] = (dq * scale).astype(jnp.bfloat16)

    @pl.when(b == 0)
    def _():
        backward(False)

    @pl.when(b == 1)
    def _():
        backward(True)
        dkv_copy().start()

    chain_step(nm - 2)

    for off in range(1, group):
        other = lax.rem(me + off, group)
        peer = (other // nb, lax.rem(other, nb), m)
        remote(
            att_all.at[other], att_all.at[other], at_ssem.at[off], at_rsem.at[other], peer
        ).wait_recv()
        remote(
            cot_cols.at[other], cot_cols.at[other], cc_ssem.at[0, 0], cc_rsem.at[other], peer
        ).wait_recv()
    own_copy(0).wait()
    dw_ref[...] = dot(
        att_all[...].reshape(group * rows, width), cot_cols[...].reshape(group * rows, half), TN
    )

    @pl.when(b == 0)
    def _():
        dkv_copy().wait_recv()
        dk_ref[0] = (dkv_own[0] + dkv_recv[0].astype(jnp.float32)).astype(jnp.bfloat16)
        dv_ref[0] = (dkv_own[1] + dkv_recv[1].astype(jnp.float32)).astype(jnp.bfloat16)

    for c in range(chunks):
        mine = partial(m, c)
        at = slice(c * part, (c + 1) * part)

        @pl.when(m > 0)
        def _():
            sum_up(m, c).wait_recv()

        @pl.when(m < nm - 1)
        def _():
            sum_down(m, c).wait_recv()

        @pl.when(m == 0)
        def _():
            mixed_ref[0, :, at] = (mine + down_in[m, c].astype(jnp.float32)).astype(jnp.bfloat16)

        @pl.when(m == nm - 1)
        def _():
            mixed_ref[0, :, at] = (mine + up_in[m, c].astype(jnp.float32)).astype(jnp.bfloat16)

        @pl.when(jnp.logical_and(m > 0, m < nm - 1))
        def _():
            mixed_ref[0, :, at] = (
                mine + up_in[m, c].astype(jnp.float32) + down_in[m, c].astype(jnp.float32)
            ).astype(jnp.bfloat16)

    for shard in range(nm):
        @pl.when(jnp.logical_and(m < nm - 1, shard <= m))
        def _():
            gather_up(shard).wait_send()

        @pl.when(jnp.logical_and(m > 0, shard >= m))
        def _():
            gather_down(shard).wait_send()

        for to_b in range(nb):
            @pl.when(jnp.logical_not(jnp.logical_and(shard == d, b == to_b)))
            def _():
                column_copy(shard, to_b).wait_send()

        for c in range(chunks):
            @pl.when(shard > m)
            def _():
                sum_up(shard, c).wait_send()

            @pl.when(shard < m)
            def _():
                sum_down(shard, c).wait_send()

    for off in range(1, group):
        att_copy(off).wait_send()

    @pl.when(b == 0)
    def _():
        for copy in kv_copies():
            copy.wait_send()

    @pl.when(b == 1)
    def _():
        dkv_copy().wait_send()


def fused(nd, nm, queries, keys, values, clip_ids, w_out, cotangent):
    nb, chunks = 2, 2
    group = nd * nb
    _, rows, width = queries.shape
    piece = cotangent.shape[2]
    half, part = piece // nb, piece // chunks
    heads = width // HD
    lanes = -(-rows // 128) * 128
    bf16, f32 = jnp.bfloat16, jnp.float32
    dma = pltpu.SemaphoreType.DMA
    vmem = pl.BlockSpec(memory_space=pltpu.VMEM)
    return pl.pallas_call(
        functools.partial(fused_kernel, nd, nm, chunks),
        out_shape=(
            jax.ShapeDtypeStruct((1, rows, piece), bf16),
            jax.ShapeDtypeStruct((1, rows, width), bf16),
            jax.ShapeDtypeStruct((1, rows, width), bf16),
            jax.ShapeDtypeStruct((1, rows, width), bf16),
            jax.ShapeDtypeStruct((width, half), f32),
        ),
        in_specs=[vmem] * 4 + [pl.BlockSpec(memory_space=pl.ANY), vmem],
        out_specs=(vmem,) * 5,
        scratch_shapes=[
            pltpu.VMEM(w_out.shape, bf16),
            pltpu.VMEM((nm, rows, piece), bf16),
            pltpu.VMEM((group, rows, half), bf16),
            pltpu.VMEM((group, rows, width), bf16),
            pltpu.VMEM((2, rows, width), bf16),
            pltpu.VMEM((8, lanes), jnp.int32),
            pltpu.VMEM((8, lanes), jnp.int32),
            pltpu.VMEM((heads, rows, rows), f32),
            pltpu.VMEM((heads, rows, rows), f32),
            pltpu.VMEM((rows, width), bf16),
            pltpu.VMEM((2, rows, width), f32),
            pltpu.VMEM((2, rows, width), bf16),
            pltpu.VMEM((2, rows, width), bf16),
            pltpu.VMEM((nm, chunks, rows, part), bf16),
            pltpu.VMEM((nm, chunks, rows, part), bf16),
            pltpu.VMEM((nm, chunks, rows, part), bf16),
            pltpu.VMEM((nm, chunks, rows, part), bf16),
            dma, dma, dma((3,)), dma((3,)), dma((nm,)), dma((nm,)), dma((nm,)),
            dma((nm, nb)), dma((group,)), dma((group,)), dma((group,)),
            dma((nm, chunks)), dma((nm, chunks)), dma((nm, chunks)), dma((nm, chunks)), dma, dma,
        ],
        compiler_params=pltpu.CompilerParams(
            collective_id=0, has_side_effects=True, vmem_limit_bytes=48 * 1024 * 1024
        ),
    )(queries, keys, values, clip_ids, w_out, cotangent)


def seen_mask(q_pos, q_clip, k_pos, k_clip):
    return (k_pos[None, :] <= q_pos[:, None]) & (k_clip[None, :] == q_clip[:, None])


def per_device(queries, keys, values, clip_ids, w_out, cotangent):
    q_here = queries[0]
    k_here = keys[0]
    v_here = values[0]
    rows = q_here.shape[0]
    width = q_here.shape[1]
    heads = width // HD
    scale = HD ** (-0.5)
    first = lax.axis_index("blk") * rows
    q_pos = first + jnp.arange(rows, dtype=jnp.int32)
    clips_all = lax.all_gather(clip_ids[0], "blk", axis=0, tiled=True)
    clip_here = lax.dynamic_slice_in_dim(clips_all, first, rows, 0)
    qh = q_here.reshape(rows, heads, HD)
    kh = k_here.reshape(rows, heads, HD)
    vh = v_here.reshape(rows, heads, HD)
    k_piece = lax.all_gather(k_here, "blk", axis=0, tiled=True)
    v_piece = lax.all_gather(v_here, "blk", axis=0, tiled=True)
    count = k_piece.shape[0]
    k_pos = jnp.arange(count, dtype=jnp.int32)
    k_clip = clips_all
    allowed = seen_mask(q_pos, clip_here, k_pos, k_clip)
    peak = jnp.full((heads, rows), NEG, jnp.float32)
    accum = jnp.zeros((rows, heads, HD), jnp.float32)
    scores = (
        jnp.einsum(
            "qhd,khd->hqk",
            qh,
            k_piece.reshape(count, heads, HD),
            preferred_element_type=jnp.float32,
        )
        * scale
    )
    scores = jnp.where(allowed[None], scores, NEG)
    new_peak = jnp.maximum(peak, jnp.max(scores, axis=-1))
    factor = jnp.exp(peak - new_peak)
    probs = jnp.where(allowed[None], jnp.exp(scores - new_peak[:, :, None]), 0.0)
    total = jnp.sum(probs, axis=-1)
    v_block = v_piece.reshape(count, heads, HD).astype(jnp.float32)
    accum = accum * factor.T[:, :, None] + jnp.einsum(
        "hqk,khd->qhd",
        probs,
        v_block,
        precision=lax.Precision.HIGHEST,
        preferred_element_type=jnp.float32,
    )
    peak, total, accum = (new_peak, total, accum)
    lse = peak + jnp.log(total)
    attended = (accum / total.T[:, :, None]).astype(jnp.bfloat16).reshape(rows, width)
    partial_value = jnp.dot(attended, w_out, preferred_element_type=jnp.float32)
    mixed = lax.psum_scatter(partial_value, "mp", scatter_dimension=1, tiled=True).astype(
        jnp.bfloat16
    )
    cot_full = lax.all_gather(cotangent[0], "mp", axis=1, tiled=True)
    d_att = lax.dot_general(
        cot_full, w_out, (((1,), (1,)), ((), ())), preferred_element_type=jnp.float32
    ).astype(jnp.bfloat16)
    doh = d_att.reshape(rows, heads, HD)
    delta = jnp.sum(
        doh.astype(jnp.float32) * attended.reshape(rows, heads, HD).astype(jnp.float32), axis=-1
    )
    lse_all, delta_all = (
        lax.all_gather(lse.T, "blk", axis=0, tiled=True),
        lax.all_gather(delta, "blk", axis=0, tiled=True),
    )
    k_piece = lax.all_gather(k_here, "blk", axis=0, tiled=True)
    v_piece = lax.all_gather(v_here, "blk", axis=0, tiled=True)
    count = k_piece.shape[0]
    k_pos = jnp.arange(count, dtype=jnp.int32)
    k_clip = clips_all
    allowed = seen_mask(q_pos, clip_here, k_pos, k_clip)
    k_heads = k_piece.reshape(count, heads, HD)
    scores = jnp.einsum("qhd,khd->hqk", qh, k_heads, preferred_element_type=jnp.float32) * scale
    probs = jnp.where(
        allowed[None], jnp.exp(jnp.where(allowed[None], scores, NEG) - lse[:, :, None]), 0.0
    )
    d_probs = jnp.einsum(
        "qhd,khd->hqk", doh, v_piece.reshape(count, heads, HD), preferred_element_type=jnp.float32
    )
    d_scores = (probs * (d_probs - delta.T[:, :, None])).astype(jnp.bfloat16)
    dq_sum = jnp.einsum("hqk,khd->qhd", d_scores, k_heads, preferred_element_type=jnp.float32)
    q_piece = lax.all_gather(q_here, "blk", axis=0, tiled=True)
    do_piece = lax.all_gather(d_att, "blk", axis=0, tiled=True)
    count = q_piece.shape[0]
    p_pos = jnp.arange(count, dtype=jnp.int32)
    allowed = seen_mask(p_pos, clips_all, q_pos, clip_here)
    q_heads = q_piece.reshape(count, heads, HD)
    do_heads = do_piece.reshape(count, heads, HD)
    scores = jnp.einsum("qhd,khd->hqk", q_heads, kh, preferred_element_type=jnp.float32) * scale
    probs = jnp.where(
        allowed[None], jnp.exp(jnp.where(allowed[None], scores, NEG) - lse_all.T[:, :, None]), 0.0
    )
    dv_acc = jnp.einsum(
        "hqk,qhd->khd", probs.astype(jnp.bfloat16), do_heads, preferred_element_type=jnp.float32
    )
    d_probs = jnp.einsum("qhd,khd->hqk", do_heads, vh, preferred_element_type=jnp.float32)
    d_scores = (probs * (d_probs - delta_all.T[:, :, None])).astype(jnp.bfloat16)
    dk_acc = jnp.einsum("hqk,qhd->khd", d_scores, q_heads, preferred_element_type=jnp.float32)
    d_queries = (dq_sum * scale).astype(jnp.bfloat16).reshape(1, rows, width)
    d_keys = (dk_acc * scale).astype(jnp.bfloat16).reshape(1, rows, width)
    d_values = dv_acc.astype(jnp.bfloat16).reshape(1, rows, width)
    local_grad = lax.dot_general(
        attended, cot_full, (((0,), (0,)), ((), ())), preferred_element_type=jnp.float32
    )
    d_w_out = lax.psum_scatter(local_grad, ("dp", "blk"), scatter_dimension=1, tiled=True)
    return (mixed[None], d_queries, d_keys, d_values, d_w_out)


def solution(mesh):
    placed = (
        P("dp", "blk", "mp"),
        P("dp", "blk", "mp"),
        P("dp", "blk", "mp"),
        P("dp", "blk"),
        P("mp", None),
        P("dp", "blk", "mp"),
    )
    nd, nb, nm = mesh.shape["dp"], mesh.shape["blk"], mesh.shape["mp"]
    body = per_device
    if nb == 2 and nd == nm:
        body = functools.partial(fused, nd, nm)
    return jax.shard_map(
        body,
        mesh=mesh,
        in_specs=placed,
        out_specs=(
            P("dp", "blk", "mp"),
            P("dp", "blk", "mp"),
            P("dp", "blk", "mp"),
            P("dp", "blk", "mp"),
            P("mp", ("dp", "blk")),
        ),
        check_vma=False,
    )
```

```python
import functools

import jax
import jax.numpy as jnp
from jax import lax
from jax.experimental import pallas as pl
from jax.experimental.pallas import tpu as pltpu
from jax.sharding import PartitionSpec as P

HD = 128
NEG = -1e30
MESH = pl.DeviceIdType.MESH
NN = (((1,), (0,)), ((), ()))
NT = (((1,), (1,)), ((), ()))
TN = (((0,), (0,)), ((), ()))


def dot(a, b, dims):
    return lax.dot_general(a, b, dims, preferred_element_type=jnp.float32)


def fused_kernel(
    nd, nm, chunks,
    q_hbm, k_hbm, v_hbm, clip_hbm, w_hbm, cot_hbm,
    mixed_ref, dq_ref, dk_ref, dv_ref, dw_ref,
    q_ref, k_ref, v_ref, clip_ref, w_ref, cot_full, cot_cols, att_all, kv_prev, clip_send, clip_prev,
    p_own, p_prev, d_att, dkv_own, dkv_send, dkv_recv,
    up_out, up_in, down_out, down_in,
    in_sem, w_sem, own_sem, kv_ssem, kv_rsem, ag_up_ssem, ag_dn_ssem, ag_rsem,
    cc_ssem, cc_rsem, at_ssem, at_rsem,
    up_ssem, up_rsem, dn_ssem, dn_rsem, dkv_ssem, dkv_rsem,
):
    nb = 2
    d, b, m = lax.axis_index("dp"), lax.axis_index("blk"), lax.axis_index("mp")
    me = d * nb + b
    group = nd * nb
    rows, width = q_ref.shape[1], q_ref.shape[2]
    heads = width // HD
    scale = HD ** (-0.5)
    piece = cot_full.shape[2]
    half = piece // nb
    part = piece // chunks

    def remote(src, dst, ssem, rsem, device):
        return pltpu.make_async_remote_copy(
            src_ref=src, dst_ref=dst, send_sem=ssem, recv_sem=rsem,
            device_id=device, device_id_type=MESH,
        )

    w_copy = pltpu.make_async_copy(w_hbm, w_ref, w_sem)
    fetches = [
        pltpu.make_async_copy(src, dst, in_sem.at[i])
        for i, (src, dst) in enumerate((
            (cot_hbm.at[0], cot_full.at[m]), (k_hbm, k_ref), (v_hbm, v_ref), (q_hbm, q_ref),
            (clip_hbm, clip_ref),
        ))
    ]
    for copy in fetches:
        copy.start()
    w_copy.start()

    barrier = pltpu.get_barrier_semaphore()
    for off in range(1, group):
        other = lax.rem(me + off, group)
        pl.semaphore_signal(
            barrier, inc=1, device_id=(other // nb, lax.rem(other, nb), m), device_id_type=MESH
        )

    @pl.when(m > 0)
    def _():
        pl.semaphore_signal(barrier, inc=1, device_id=(d, b, m - 1), device_id_type=MESH)

    @pl.when(m < nm - 1)
    def _():
        pl.semaphore_signal(barrier, inc=1, device_id=(d, b, m + 1), device_id_type=MESH)

    clip_send[...] = jnp.zeros_like(clip_send)
    for copy in fetches:
        copy.wait()
    clip_send[0:1, 0:rows] = clip_ref[...]
    pl.semaphore_wait(
        barrier, group - 1 + jnp.where(m > 0, 1, 0) + jnp.where(m < nm - 1, 1, 0)
    )

    def kv_copies():
        peer = (d, 1, m)
        return (
            remote(k_ref.at[0], kv_prev.at[0], kv_ssem.at[0], kv_rsem.at[0], peer),
            remote(v_ref.at[0], kv_prev.at[1], kv_ssem.at[1], kv_rsem.at[1], peer),
            remote(clip_send, clip_prev, kv_ssem.at[2], kv_rsem.at[2], peer),
        )

    def gather_up(shard):
        return remote(
            cot_full.at[shard], cot_full.at[shard], ag_up_ssem.at[shard], ag_rsem.at[shard],
            (d, b, m + 1),
        )

    def gather_down(shard):
        return remote(
            cot_full.at[shard], cot_full.at[shard], ag_dn_ssem.at[shard], ag_rsem.at[shard],
            (d, b, m - 1),
        )

    def column_copy(shard, to_b):
        return remote(
            cot_full.at[shard, :, pl.ds(to_b * half, half)], cot_cols.at[me],
            cc_ssem.at[shard, to_b], cc_rsem.at[me], (shard, to_b, m),
        )

    def own_copy(to_b):
        return pltpu.make_async_copy(
            cot_full.at[d, :, pl.ds(to_b * half, half)], cot_cols.at[me], own_sem
        )

    def each_column(shard, away, here):
        for to_b in range(nb):
            is_me = jnp.logical_and(shard == d, b == to_b)

            @pl.when(jnp.logical_not(is_me))
            def _():
                away(column_copy(shard, to_b))

            @pl.when(is_me)
            def _():
                here(own_copy(to_b))

    def start(copy):
        copy.start()

    @pl.when(m < nm - 1)
    def _():
        gather_up(m).start()

    @pl.when(m > 0)
    def _():
        gather_down(m).start()

    @pl.when(b == 0)
    def _():
        for copy in kv_copies():
            copy.start()

    @pl.when(b == 1)
    def _():
        each_column(m, start, start)

    def gather_step(step):
        @pl.when(m - step >= 0)
        def _():
            shard = m - step
            gather_down(shard).wait_recv()

            @pl.when(m < nm - 1)
            def _():
                gather_up(shard).start()

            each_column(shard, start, start)

        @pl.when(m + step < nm)
        def _():
            shard = m + step
            gather_up(shard).wait_recv()

            @pl.when(m > 0)
            def _():
                gather_down(shard).start()

            each_column(shard, start, start)

    row = lax.broadcasted_iota(jnp.int32, (rows, rows), 0)
    col = lax.broadcasted_iota(jnp.int32, (rows, rows), 1)

    def clip_rows(ref):
        return jnp.broadcast_to(ref[0:1, 0:rows], (rows, rows))

    def own_scores(h):
        cols = pl.ds(h * HD, HD)
        return jnp.where(seen, dot(q_ref[0, :, cols], k_ref[0, :, cols], NT) * scale, NEG)

    here = clip_rows(clip_send)
    mine = jnp.sum(jnp.where(row == col, here, 0), axis=1, keepdims=True)
    seen = jnp.logical_and(col <= row, here == mine)

    @pl.when(b == 0)
    def _():
        for h in range(heads):
            cols = pl.ds(h * HD, HD)
            s = own_scores(h)
            e = jnp.exp(s - jnp.max(s, axis=1, keepdims=True))
            e = e * (1.0 / jnp.sum(e, axis=1, keepdims=True))
            p_own[h] = e
            att = dot(e.astype(jnp.bfloat16), v_ref[0, :, cols], NN)
            att_all[me, :, cols] = att.astype(jnp.bfloat16)

    @pl.when(b == 1)
    def _():
        for h in range(heads):
            p_own[h] = own_scores(h)

    gather_step(1)

    @pl.when(b == 0)
    def _():
        each_column(m, start, start)

    @pl.when(b == 1)
    def _():
        k_copy, v_copy, clip_copy = kv_copies()
        clip_copy.wait_recv()
        k_copy.wait_recv()
        earlier = clip_rows(clip_prev) == mine
        for h in range(heads):
            cols = pl.ds(h * HD, HD)
            s = p_own[h]
            t = jnp.where(
                earlier, dot(q_ref[0, :, cols], kv_prev[0, :, cols], NT) * scale, NEG
            )
            peak = jnp.maximum(
                jnp.max(s, axis=1, keepdims=True), jnp.max(t, axis=1, keepdims=True)
            )
            e, f = jnp.exp(s - peak), jnp.exp(t - peak)
            inverse = 1.0 / (
                jnp.sum(e, axis=1, keepdims=True) + jnp.sum(f, axis=1, keepdims=True)
            )
            e, f = e * inverse, f * inverse
            p_own[h] = e
            p_prev[h] = f
            dkv_own[0, :, cols] = dot(e.astype(jnp.bfloat16), v_ref[0, :, cols], NN)
        v_copy.wait_recv()
        for h in range(heads):
            cols = pl.ds(h * HD, HD)
            att = dkv_own[0, :, cols] + dot(
                p_prev[h].astype(jnp.bfloat16), kv_prev[1, :, cols], NN
            )
            att_all[me, :, cols] = att.astype(jnp.bfloat16)

    pairs = group // 2
    core = lax.rem(d, 2)
    partner = (d + 1 - 2 * core, b, m)
    pair = (d // 2) * nb + b

    def att_slot(off):
        other = lax.rem(pair + off, pairs)
        return (other // nb) * 2 + core, lax.rem(other, nb)

    def att_copy(off):
        to_d, to_b = att_slot(off)
        return remote(
            att_all.at[me], att_all.at[me], at_ssem.at[off], at_rsem.at[me], (to_d, to_b, m)
        )

    def att_pass(off):
        of_d, of_b = att_slot(off)
        slot = of_d * nb + of_b
        return remote(
            att_all.at[slot], att_all.at[slot], at_ssem.at[pairs + off], at_rsem.at[slot], partner
        )

    for off in range(1, pairs):
        att_copy(off).start()
    att_pass(0).start()

    w_copy.wait()

    def partial(dest, c):
        at = pl.multiple_of(dest * piece + c * part, part)
        return dot(att_all[me], w_ref[:, pl.ds(at, part)], NN)

    def sum_up(dest, c):
        return remote(
            up_out.at[dest, c], up_in.at[dest, c], up_ssem.at[dest, c], up_rsem.at[dest, c],
            (d, b, m + 1),
        )

    def sum_down(dest, c):
        return remote(
            down_out.at[dest, c], down_in.at[dest, c], dn_ssem.at[dest, c], dn_rsem.at[dest, c],
            (d, b, m - 1),
        )

    def chain_step(step):
        for c in range(chunks):
            @pl.when(step >= m)
            def _():
                dest = nm - 1 - step + m
                mine = partial(dest, c)

                @pl.when(m == 0)
                def _():
                    up_out[dest, c] = mine.astype(jnp.bfloat16)

                @pl.when(m > 0)
                def _():
                    sum_up(dest, c).wait_recv()
                    up_out[dest, c] = (
                        mine + up_in[dest, c].astype(jnp.float32)
                    ).astype(jnp.bfloat16)

                sum_up(dest, c).start()

            @pl.when(step >= nm - 1 - m)
            def _():
                dest = step - (nm - 1 - m)
                mine = partial(dest, c)

                @pl.when(m == nm - 1)
                def _():
                    down_out[dest, c] = mine.astype(jnp.bfloat16)

                @pl.when(m < nm - 1)
                def _():
                    sum_down(dest, c).wait_recv()
                    down_out[dest, c] = (
                        mine + down_in[dest, c].astype(jnp.float32)
                    ).astype(jnp.bfloat16)

                sum_down(dest, c).start()

    for step in range(nm - 2):
        chain_step(step)
        gather_step(step + 2)

    total = dot(cot_full[0], w_ref[:, 0:piece], NT)
    for shard in range(1, nm):
        total = total + dot(cot_full[shard], w_ref[:, shard * piece:(shard + 1) * piece], NT)
    d_att[...] = total.astype(jnp.bfloat16)

    def dkv_copy():
        return remote(dkv_send, dkv_recv, dkv_ssem, dkv_rsem, (d, 0, m))

    def backward(use_prev):
        for h in range(heads):
            cols = pl.ds(h * HD, HD)
            do = d_att[:, cols]
            q = q_ref[0, :, cols]
            delta = jnp.sum(
                do.astype(jnp.float32) * att_all[me, :, cols].astype(jnp.float32),
                axis=1, keepdims=True,
            )
            e = p_own[h]
            ds = (e * (dot(do, v_ref[0, :, cols], NT) - delta)).astype(jnp.bfloat16)
            dq = dot(ds, k_ref[0, :, cols], NN)
            dk = dot(ds, q, TN) * scale
            dv = dot(e.astype(jnp.bfloat16), do, TN)
            if use_prev:
                f = p_prev[h]
                dt = (f * (dot(do, kv_prev[1, :, cols], NT) - delta)).astype(jnp.bfloat16)
                dq = dq + dot(dt, kv_prev[0, :, cols], NN)
                dkv_send[0, :, cols] = (dot(dt, q, TN) * scale).astype(jnp.bfloat16)
                dkv_send[1, :, cols] = dot(f.astype(jnp.bfloat16), do, TN).astype(jnp.bfloat16)
                dk_ref[0, :, cols] = dk.astype(jnp.bfloat16)
                dv_ref[0, :, cols] = dv.astype(jnp.bfloat16)
            else:
                dkv_own[0, :, cols] = dk
                dkv_own[1, :, cols] = dv
            dq_ref[0, :, cols] = (dq * scale).astype(jnp.bfloat16)

    @pl.when(b == 0)
    def _():
        backward(False)

    @pl.when(b == 1)
    def _():
        backward(True)
        dkv_copy().start()

    chain_step(nm - 2)

    for off in range(1, pairs):
        att_pass(off).wait_recv()
        att_pass(off).start()

    for off in range(pairs):
        of_d, of_b = att_slot(off)
        slot = (of_d + 1 - 2 * core) * nb + of_b
        remote(
            att_all.at[slot], att_all.at[slot], at_ssem.at[0], at_rsem.at[slot], partner
        ).wait_recv()
    for off in range(1, group):
        other = lax.rem(me + off, group)
        remote(
            cot_cols.at[other], cot_cols.at[other], cc_ssem.at[0, 0], cc_rsem.at[other], partner
        ).wait_recv()
    own_copy(0).wait()
    dw_ref[...] = dot(
        att_all[...].reshape(group * rows, width), cot_cols[...].reshape(group * rows, half), TN
    )

    @pl.when(b == 0)
    def _():
        dkv_copy().wait_recv()
        dk_ref[0] = (dkv_own[0] + dkv_recv[0].astype(jnp.float32)).astype(jnp.bfloat16)
        dv_ref[0] = (dkv_own[1] + dkv_recv[1].astype(jnp.float32)).astype(jnp.bfloat16)

    for c in range(chunks):
        mine = partial(m, c)
        at = slice(c * part, (c + 1) * part)

        @pl.when(m > 0)
        def _():
            sum_up(m, c).wait_recv()

        @pl.when(m < nm - 1)
        def _():
            sum_down(m, c).wait_recv()

        @pl.when(m == 0)
        def _():
            mixed_ref[0, :, at] = (mine + down_in[m, c].astype(jnp.float32)).astype(jnp.bfloat16)

        @pl.when(m == nm - 1)
        def _():
            mixed_ref[0, :, at] = (mine + up_in[m, c].astype(jnp.float32)).astype(jnp.bfloat16)

        @pl.when(jnp.logical_and(m > 0, m < nm - 1))
        def _():
            mixed_ref[0, :, at] = (
                mine + up_in[m, c].astype(jnp.float32) + down_in[m, c].astype(jnp.float32)
            ).astype(jnp.bfloat16)

    for shard in range(nm):
        @pl.when(jnp.logical_and(m < nm - 1, shard <= m))
        def _():
            gather_up(shard).wait_send()

        @pl.when(jnp.logical_and(m > 0, shard >= m))
        def _():
            gather_down(shard).wait_send()

        for to_b in range(nb):
            @pl.when(jnp.logical_not(jnp.logical_and(shard == d, b == to_b)))
            def _():
                column_copy(shard, to_b).wait_send()

        for c in range(chunks):
            @pl.when(shard > m)
            def _():
                sum_up(shard, c).wait_send()

            @pl.when(shard < m)
            def _():
                sum_down(shard, c).wait_send()

    for off in range(1, pairs):
        att_copy(off).wait_send()
    for off in range(pairs):
        att_pass(off).wait_send()

    @pl.when(b == 0)
    def _():
        for copy in kv_copies():
            copy.wait_send()

    @pl.when(b == 1)
    def _():
        dkv_copy().wait_send()


def write_kernel(*refs):
    sem = refs[10]
    copies = [pltpu.make_async_copy(refs[i], refs[5 + i], sem.at[i]) for i in range(5)]
    for copy in copies:
        copy.start()
    for copy in copies:
        copy.wait()


def fused(nd, nm, queries, keys, values, clip_ids, w_out, cotangent):
    nb, chunks = 2, 2
    group = nd * nb
    _, rows, width = queries.shape
    piece = cotangent.shape[2]
    half, part = piece // nb, piece // chunks
    heads = width // HD
    lanes = -(-rows // 128) * 128
    bf16, f32 = jnp.bfloat16, jnp.float32
    dma = pltpu.SemaphoreType.DMA
    vmem = pl.BlockSpec(memory_space=pltpu.VMEM)
    results = pl.pallas_call(
        functools.partial(fused_kernel, nd, nm, chunks),
        out_shape=(
            jax.ShapeDtypeStruct((1, rows, piece), bf16),
            jax.ShapeDtypeStruct((1, rows, width), bf16),
            jax.ShapeDtypeStruct((1, rows, width), bf16),
            jax.ShapeDtypeStruct((1, rows, width), bf16),
            jax.ShapeDtypeStruct((width, half), f32),
        ),
        in_specs=[pl.BlockSpec(memory_space=pltpu.HBM)] * 6,
        out_specs=(vmem,) * 5,
        scratch_shapes=[
            pltpu.VMEM(queries.shape, bf16),
            pltpu.VMEM(queries.shape, bf16),
            pltpu.VMEM(queries.shape, bf16),
            pltpu.VMEM(clip_ids.shape, jnp.int32),
            pltpu.VMEM(w_out.shape, bf16),
            pltpu.VMEM((nm, rows, piece), bf16),
            pltpu.VMEM((group, rows, half), bf16),
            pltpu.VMEM((group, rows, width), bf16),
            pltpu.VMEM((2, rows, width), bf16),
            pltpu.VMEM((8, lanes), jnp.int32),
            pltpu.VMEM((8, lanes), jnp.int32),
            pltpu.VMEM((heads, rows, rows), f32),
            pltpu.VMEM((heads, rows, rows), f32),
            pltpu.VMEM((rows, width), bf16),
            pltpu.VMEM((2, rows, width), f32),
            pltpu.VMEM((2, rows, width), bf16),
            pltpu.VMEM((2, rows, width), bf16),
            pltpu.VMEM((nm, chunks, rows, part), bf16),
            pltpu.VMEM((nm, chunks, rows, part), bf16),
            pltpu.VMEM((nm, chunks, rows, part), bf16),
            pltpu.VMEM((nm, chunks, rows, part), bf16),
            dma((5,)), dma, dma, dma((3,)), dma((3,)), dma((nm,)), dma((nm,)), dma((nm,)),
            dma((nm, nb)), dma((group,)), dma((group,)), dma((group,)),
            dma((nm, chunks)), dma((nm, chunks)), dma((nm, chunks)), dma((nm, chunks)), dma, dma,
        ],
        compiler_params=pltpu.CompilerParams(
            collective_id=0, has_side_effects=True, vmem_limit_bytes=61 * 1024 * 1024
        ),
    )(queries, keys, values, clip_ids, w_out, cotangent)
    return pl.pallas_call(
        write_kernel,
        out_shape=tuple(jax.ShapeDtypeStruct(x.shape, x.dtype) for x in results),
        in_specs=[pl.BlockSpec(memory_space=pltpu.HBM)] * 5,
        out_specs=(pl.BlockSpec(memory_space=pltpu.HBM),) * 5,
        scratch_shapes=[dma((5,))],
        compiler_params=pltpu.CompilerParams(vmem_limit_bytes=61 * 1024 * 1024),
    )(*results)


def seen_mask(q_pos, q_clip, k_pos, k_clip):
    return (k_pos[None, :] <= q_pos[:, None]) & (k_clip[None, :] == q_clip[:, None])


def per_device(queries, keys, values, clip_ids, w_out, cotangent):
    q_here = queries[0]
    k_here = keys[0]
    v_here = values[0]
    rows = q_here.shape[0]
    width = q_here.shape[1]
    heads = width // HD
    scale = HD ** (-0.5)
    first = lax.axis_index("blk") * rows
    q_pos = first + jnp.arange(rows, dtype=jnp.int32)
    clips_all = lax.all_gather(clip_ids[0], "blk", axis=0, tiled=True)
    clip_here = lax.dynamic_slice_in_dim(clips_all, first, rows, 0)
    qh = q_here.reshape(rows, heads, HD)
    kh = k_here.reshape(rows, heads, HD)
    vh = v_here.reshape(rows, heads, HD)
    k_piece = lax.all_gather(k_here, "blk", axis=0, tiled=True)
    v_piece = lax.all_gather(v_here, "blk", axis=0, tiled=True)
    count = k_piece.shape[0]
    k_pos = jnp.arange(count, dtype=jnp.int32)
    k_clip = clips_all
    allowed = seen_mask(q_pos, clip_here, k_pos, k_clip)
    peak = jnp.full((heads, rows), NEG, jnp.float32)
    accum = jnp.zeros((rows, heads, HD), jnp.float32)
    scores = (
        jnp.einsum(
            "qhd,khd->hqk",
            qh,
            k_piece.reshape(count, heads, HD),
            preferred_element_type=jnp.float32,
        )
        * scale
    )
    scores = jnp.where(allowed[None], scores, NEG)
    new_peak = jnp.maximum(peak, jnp.max(scores, axis=-1))
    factor = jnp.exp(peak - new_peak)
    probs = jnp.where(allowed[None], jnp.exp(scores - new_peak[:, :, None]), 0.0)
    total = jnp.sum(probs, axis=-1)
    v_block = v_piece.reshape(count, heads, HD).astype(jnp.float32)
    accum = accum * factor.T[:, :, None] + jnp.einsum(
        "hqk,khd->qhd",
        probs,
        v_block,
        precision=lax.Precision.HIGHEST,
        preferred_element_type=jnp.float32,
    )
    peak, total, accum = (new_peak, total, accum)
    lse = peak + jnp.log(total)
    attended = (accum / total.T[:, :, None]).astype(jnp.bfloat16).reshape(rows, width)
    partial_value = jnp.dot(attended, w_out, preferred_element_type=jnp.float32)
    mixed = lax.psum_scatter(partial_value, "mp", scatter_dimension=1, tiled=True).astype(
        jnp.bfloat16
    )
    cot_full = lax.all_gather(cotangent[0], "mp", axis=1, tiled=True)
    d_att = lax.dot_general(
        cot_full, w_out, (((1,), (1,)), ((), ())), preferred_element_type=jnp.float32
    ).astype(jnp.bfloat16)
    doh = d_att.reshape(rows, heads, HD)
    delta = jnp.sum(
        doh.astype(jnp.float32) * attended.reshape(rows, heads, HD).astype(jnp.float32), axis=-1
    )
    lse_all, delta_all = (
        lax.all_gather(lse.T, "blk", axis=0, tiled=True),
        lax.all_gather(delta, "blk", axis=0, tiled=True),
    )
    k_piece = lax.all_gather(k_here, "blk", axis=0, tiled=True)
    v_piece = lax.all_gather(v_here, "blk", axis=0, tiled=True)
    count = k_piece.shape[0]
    k_pos = jnp.arange(count, dtype=jnp.int32)
    k_clip = clips_all
    allowed = seen_mask(q_pos, clip_here, k_pos, k_clip)
    k_heads = k_piece.reshape(count, heads, HD)
    scores = jnp.einsum("qhd,khd->hqk", qh, k_heads, preferred_element_type=jnp.float32) * scale
    probs = jnp.where(
        allowed[None], jnp.exp(jnp.where(allowed[None], scores, NEG) - lse[:, :, None]), 0.0
    )
    d_probs = jnp.einsum(
        "qhd,khd->hqk", doh, v_piece.reshape(count, heads, HD), preferred_element_type=jnp.float32
    )
    d_scores = (probs * (d_probs - delta.T[:, :, None])).astype(jnp.bfloat16)
    dq_sum = jnp.einsum("hqk,khd->qhd", d_scores, k_heads, preferred_element_type=jnp.float32)
    q_piece = lax.all_gather(q_here, "blk", axis=0, tiled=True)
    do_piece = lax.all_gather(d_att, "blk", axis=0, tiled=True)
    count = q_piece.shape[0]
    p_pos = jnp.arange(count, dtype=jnp.int32)
    allowed = seen_mask(p_pos, clips_all, q_pos, clip_here)
    q_heads = q_piece.reshape(count, heads, HD)
    do_heads = do_piece.reshape(count, heads, HD)
    scores = jnp.einsum("qhd,khd->hqk", q_heads, kh, preferred_element_type=jnp.float32) * scale
    probs = jnp.where(
        allowed[None], jnp.exp(jnp.where(allowed[None], scores, NEG) - lse_all.T[:, :, None]), 0.0
    )
    dv_acc = jnp.einsum(
        "hqk,qhd->khd", probs.astype(jnp.bfloat16), do_heads, preferred_element_type=jnp.float32
    )
    d_probs = jnp.einsum("qhd,khd->hqk", do_heads, vh, preferred_element_type=jnp.float32)
    d_scores = (probs * (d_probs - delta_all.T[:, :, None])).astype(jnp.bfloat16)
    dk_acc = jnp.einsum("hqk,qhd->khd", d_scores, q_heads, preferred_element_type=jnp.float32)
    d_queries = (dq_sum * scale).astype(jnp.bfloat16).reshape(1, rows, width)
    d_keys = (dk_acc * scale).astype(jnp.bfloat16).reshape(1, rows, width)
    d_values = dv_acc.astype(jnp.bfloat16).reshape(1, rows, width)
    local_grad = lax.dot_general(
        attended, cot_full, (((0,), (0,)), ((), ())), preferred_element_type=jnp.float32
    )
    d_w_out = lax.psum_scatter(local_grad, ("dp", "blk"), scatter_dimension=1, tiled=True)
    return (mixed[None], d_queries, d_keys, d_values, d_w_out)


def solution(mesh):
    placed = (
        P("dp", "blk", "mp"),
        P("dp", "blk", "mp"),
        P("dp", "blk", "mp"),
        P("dp", "blk"),
        P("mp", None),
        P("dp", "blk", "mp"),
    )
    nd, nb, nm = mesh.shape["dp"], mesh.shape["blk"], mesh.shape["mp"]
    body = per_device
    if nb == 2 and nd == nm and nd % 2 == 0:
        body = functools.partial(fused, nd, nm)
    return jax.shard_map(
        body,
        mesh=mesh,
        in_specs=placed,
        out_specs=(
            P("dp", "blk", "mp"),
            P("dp", "blk", "mp"),
            P("dp", "blk", "mp"),
            P("dp", "blk", "mp"),
            P("mp", ("dp", "blk")),
        ),
        check_vma=False,
    )
```

```python
import functools

import jax
import jax.numpy as jnp
from jax import lax
from jax.experimental import pallas as pl
from jax.experimental.pallas import tpu as pltpu
from jax.sharding import PartitionSpec as P

HD = 128
NEG = -1e30
MESH = pl.DeviceIdType.MESH
NN = (((1,), (0,)), ((), ()))
NT = (((1,), (1,)), ((), ()))
TN = (((0,), (0,)), ((), ()))


def dot(a, b, dims):
    return lax.dot_general(a, b, dims, preferred_element_type=jnp.float32)


def fused_kernel(
    nd, nm, chunks,
    q_hbm, k_hbm, v_hbm, clip_hbm, w_hbm, cot_hbm,
    mixed_hbm, dq_hbm, dk_hbm, dv_hbm, dw_hbm,
    mixed_ref, dq_ref, dk_ref, dv_ref, dw_ref, out_sem,
    q_ref, k_ref, v_ref, clip_ref, w_ref, cot_full, cot_cols, att_all, kv_prev, clip_send, clip_prev,
    p_own, p_prev, d_att, dkv_own, dkv_send, dkv_recv,
    up_out, up_in, down_out, down_in,
    in_sem, w_sem, own_sem, kv_ssem, kv_rsem, ag_up_ssem, ag_dn_ssem, ag_rsem,
    cc_ssem, cc_rsem, at_ssem, at_rsem,
    up_ssem, up_rsem, dn_ssem, dn_rsem, dkv_ssem, dkv_rsem,
):
    nb = 2
    d, b, m = lax.axis_index("dp"), lax.axis_index("blk"), lax.axis_index("mp")
    me = d * nb + b
    group = nd * nb
    rows, width = q_ref.shape[1], q_ref.shape[2]
    heads = width // HD
    scale = HD ** (-0.5)
    piece = cot_full.shape[2]
    half = piece // nb
    part = piece // chunks

    def remote(src, dst, ssem, rsem, device):
        return pltpu.make_async_remote_copy(
            src_ref=src, dst_ref=dst, send_sem=ssem, recv_sem=rsem,
            device_id=device, device_id_type=MESH,
        )

    w_copy = pltpu.make_async_copy(w_hbm, w_ref, w_sem)
    fetches = [
        pltpu.make_async_copy(src, dst, in_sem.at[i])
        for i, (src, dst) in enumerate((
            (cot_hbm.at[0], cot_full.at[m]), (k_hbm, k_ref), (v_hbm, v_ref), (q_hbm, q_ref),
            (clip_hbm, clip_ref),
        ))
    ]
    for copy in fetches:
        copy.start()
    w_copy.start()

    barrier = pltpu.get_barrier_semaphore()
    for off in range(1, group):
        other = lax.rem(me + off, group)
        pl.semaphore_signal(
            barrier, inc=1, device_id=(other // nb, lax.rem(other, nb), m), device_id_type=MESH
        )

    @pl.when(m > 0)
    def _():
        pl.semaphore_signal(barrier, inc=1, device_id=(d, b, m - 1), device_id_type=MESH)

    @pl.when(m < nm - 1)
    def _():
        pl.semaphore_signal(barrier, inc=1, device_id=(d, b, m + 1), device_id_type=MESH)

    clip_send[...] = jnp.zeros_like(clip_send)
    for copy in fetches:
        copy.wait()
    clip_send[0:1, 0:rows] = clip_ref[...]
    pl.semaphore_wait(
        barrier, group - 1 + jnp.where(m > 0, 1, 0) + jnp.where(m < nm - 1, 1, 0)
    )

    def kv_copies():
        peer = (d, 1, m)
        return (
            remote(k_ref.at[0], kv_prev.at[0], kv_ssem.at[0], kv_rsem.at[0], peer),
            remote(v_ref.at[0], kv_prev.at[1], kv_ssem.at[1], kv_rsem.at[1], peer),
            remote(clip_send, clip_prev, kv_ssem.at[2], kv_rsem.at[2], peer),
        )

    def gather_up(shard):
        return remote(
            cot_full.at[shard], cot_full.at[shard], ag_up_ssem.at[shard], ag_rsem.at[shard],
            (d, b, m + 1),
        )

    def gather_down(shard):
        return remote(
            cot_full.at[shard], cot_full.at[shard], ag_dn_ssem.at[shard], ag_rsem.at[shard],
            (d, b, m - 1),
        )

    def column_copy(shard, to_b):
        return remote(
            cot_full.at[shard, :, pl.ds(to_b * half, half)], cot_cols.at[me],
            cc_ssem.at[shard, to_b], cc_rsem.at[me], (shard, to_b, m),
        )

    def own_copy(to_b):
        return pltpu.make_async_copy(
            cot_full.at[d, :, pl.ds(to_b * half, half)], cot_cols.at[me], own_sem
        )

    def each_column(shard, away, here):
        for to_b in range(nb):
            is_me = jnp.logical_and(shard == d, b == to_b)

            @pl.when(jnp.logical_not(is_me))
            def _():
                away(column_copy(shard, to_b))

            @pl.when(is_me)
            def _():
                here(own_copy(to_b))

    def start(copy):
        copy.start()

    @pl.when(m < nm - 1)
    def _():
        gather_up(m).start()

    @pl.when(m > 0)
    def _():
        gather_down(m).start()

    @pl.when(b == 0)
    def _():
        for copy in kv_copies():
            copy.start()

    @pl.when(b == 1)
    def _():
        each_column(m, start, start)

    def gather_step(step):
        @pl.when(m - step >= 0)
        def _():
            shard = m - step
            gather_down(shard).wait_recv()

            @pl.when(m < nm - 1)
            def _():
                gather_up(shard).start()

            each_column(shard, start, start)

        @pl.when(m + step < nm)
        def _():
            shard = m + step
            gather_up(shard).wait_recv()

            @pl.when(m > 0)
            def _():
                gather_down(shard).start()

            each_column(shard, start, start)

    row = lax.broadcasted_iota(jnp.int32, (rows, rows), 0)
    col = lax.broadcasted_iota(jnp.int32, (rows, rows), 1)

    def clip_rows(ref):
        return jnp.broadcast_to(ref[0:1, 0:rows], (rows, rows))

    def own_scores(h):
        cols = pl.ds(h * HD, HD)
        return jnp.where(seen, dot(q_ref[0, :, cols], k_ref[0, :, cols], NT) * scale, NEG)

    here = clip_rows(clip_send)
    mine = jnp.sum(jnp.where(row == col, here, 0), axis=1, keepdims=True)
    seen = jnp.logical_and(col <= row, here == mine)

    @pl.when(b == 0)
    def _():
        for h in range(heads):
            cols = pl.ds(h * HD, HD)
            s = own_scores(h)
            e = jnp.exp(s - jnp.max(s, axis=1, keepdims=True))
            e = e * (1.0 / jnp.sum(e, axis=1, keepdims=True))
            p_own[h] = e
            att = dot(e.astype(jnp.bfloat16), v_ref[0, :, cols], NN)
            att_all[me, :, cols] = att.astype(jnp.bfloat16)

    @pl.when(b == 1)
    def _():
        for h in range(heads):
            p_own[h] = own_scores(h)

    gather_step(1)

    @pl.when(b == 0)
    def _():
        each_column(m, start, start)

    @pl.when(b == 1)
    def _():
        k_copy, v_copy, clip_copy = kv_copies()
        clip_copy.wait_recv()
        k_copy.wait_recv()
        earlier = clip_rows(clip_prev) == mine
        for h in range(heads):
            cols = pl.ds(h * HD, HD)
            s = p_own[h]
            t = jnp.where(
                earlier, dot(q_ref[0, :, cols], kv_prev[0, :, cols], NT) * scale, NEG
            )
            peak = jnp.maximum(
                jnp.max(s, axis=1, keepdims=True), jnp.max(t, axis=1, keepdims=True)
            )
            e, f = jnp.exp(s - peak), jnp.exp(t - peak)
            inverse = 1.0 / (
                jnp.sum(e, axis=1, keepdims=True) + jnp.sum(f, axis=1, keepdims=True)
            )
            e, f = e * inverse, f * inverse
            p_own[h] = e
            p_prev[h] = f
            dkv_own[0, :, cols] = dot(e.astype(jnp.bfloat16), v_ref[0, :, cols], NN)
        v_copy.wait_recv()
        for h in range(heads):
            cols = pl.ds(h * HD, HD)
            att = dkv_own[0, :, cols] + dot(
                p_prev[h].astype(jnp.bfloat16), kv_prev[1, :, cols], NN
            )
            att_all[me, :, cols] = att.astype(jnp.bfloat16)

    pairs = group // 2
    core = lax.rem(d, 2)
    partner = (d + 1 - 2 * core, b, m)
    pair = (d // 2) * nb + b

    def att_slot(off):
        other = lax.rem(pair + off, pairs)
        return (other // nb) * 2 + core, lax.rem(other, nb)

    def att_copy(off):
        to_d, to_b = att_slot(off)
        return remote(
            att_all.at[me], att_all.at[me], at_ssem.at[off], at_rsem.at[me], (to_d, to_b, m)
        )

    def att_pass(off):
        of_d, of_b = att_slot(off)
        slot = of_d * nb + of_b
        return remote(
            att_all.at[slot], att_all.at[slot], at_ssem.at[pairs + off], at_rsem.at[slot], partner
        )

    for off in range(1, pairs):
        att_copy(off).start()
    att_pass(0).start()

    w_copy.wait()

    def partial(dest, c):
        at = pl.multiple_of(dest * piece + c * part, part)
        return dot(att_all[me], w_ref[:, pl.ds(at, part)], NN)

    def sum_up(dest, c):
        return remote(
            up_out.at[dest, c], up_in.at[dest, c], up_ssem.at[dest, c], up_rsem.at[dest, c],
            (d, b, m + 1),
        )

    def sum_down(dest, c):
        return remote(
            down_out.at[dest, c], down_in.at[dest, c], dn_ssem.at[dest, c], dn_rsem.at[dest, c],
            (d, b, m - 1),
        )

    def chain_step(step):
        for c in range(chunks):
            @pl.when(step >= m)
            def _():
                dest = nm - 1 - step + m
                mine = partial(dest, c)

                @pl.when(m == 0)
                def _():
                    up_out[dest, c] = mine.astype(jnp.bfloat16)

                @pl.when(m > 0)
                def _():
                    sum_up(dest, c).wait_recv()
                    up_out[dest, c] = (
                        mine + up_in[dest, c].astype(jnp.float32)
                    ).astype(jnp.bfloat16)

                sum_up(dest, c).start()

            @pl.when(step >= nm - 1 - m)
            def _():
                dest = step - (nm - 1 - m)
                mine = partial(dest, c)

                @pl.when(m == nm - 1)
                def _():
                    down_out[dest, c] = mine.astype(jnp.bfloat16)

                @pl.when(m < nm - 1)
                def _():
                    sum_down(dest, c).wait_recv()
                    down_out[dest, c] = (
                        mine + down_in[dest, c].astype(jnp.float32)
                    ).astype(jnp.bfloat16)

                sum_down(dest, c).start()

    for step in range(nm - 2):
        chain_step(step)
        gather_step(step + 2)

    total = dot(cot_full[0], w_ref[:, 0:piece], NT)
    for shard in range(1, nm):
        total = total + dot(cot_full[shard], w_ref[:, shard * piece:(shard + 1) * piece], NT)
    d_att[...] = total.astype(jnp.bfloat16)

    def dkv_copy():
        return remote(dkv_send, dkv_recv, dkv_ssem, dkv_rsem, (d, 0, m))

    def backward(use_prev):
        for h in range(heads):
            cols = pl.ds(h * HD, HD)
            do = d_att[:, cols]
            q = q_ref[0, :, cols]
            delta = jnp.sum(
                do.astype(jnp.float32) * att_all[me, :, cols].astype(jnp.float32),
                axis=1, keepdims=True,
            )
            e = p_own[h]
            ds = (e * (dot(do, v_ref[0, :, cols], NT) - delta)).astype(jnp.bfloat16)
            dq = dot(ds, k_ref[0, :, cols], NN)
            dk = dot(ds, q, TN) * scale
            dv = dot(e.astype(jnp.bfloat16), do, TN)
            if use_prev:
                f = p_prev[h]
                dt = (f * (dot(do, kv_prev[1, :, cols], NT) - delta)).astype(jnp.bfloat16)
                dq = dq + dot(dt, kv_prev[0, :, cols], NN)
                dkv_send[0, :, cols] = (dot(dt, q, TN) * scale).astype(jnp.bfloat16)
                dkv_send[1, :, cols] = dot(f.astype(jnp.bfloat16), do, TN).astype(jnp.bfloat16)
                dk_ref[0, :, cols] = dk.astype(jnp.bfloat16)
                dv_ref[0, :, cols] = dv.astype(jnp.bfloat16)
            else:
                dkv_own[0, :, cols] = dk
                dkv_own[1, :, cols] = dv
            dq_ref[0, :, cols] = (dq * scale).astype(jnp.bfloat16)

    @pl.when(b == 0)
    def _():
        backward(False)

    @pl.when(b == 1)
    def _():
        backward(True)
        dkv_copy().start()

    stores = [
        pltpu.make_async_copy(src, dst, out_sem.at[i])
        for i, (src, dst) in enumerate((
            (mixed_ref, mixed_hbm), (dq_ref, dq_hbm), (dk_ref, dk_hbm), (dv_ref, dv_hbm),
            (dw_ref, dw_hbm),
        ))
    ]
    stores[1].start()

    chain_step(nm - 2)

    for off in range(1, pairs):
        att_pass(off).wait_recv()
        att_pass(off).start()

    for off in range(pairs):
        of_d, of_b = att_slot(off)
        slot = (of_d + 1 - 2 * core) * nb + of_b
        remote(
            att_all.at[slot], att_all.at[slot], at_ssem.at[0], at_rsem.at[slot], partner
        ).wait_recv()
    for off in range(1, group):
        other = lax.rem(me + off, group)
        remote(
            cot_cols.at[other], cot_cols.at[other], cc_ssem.at[0, 0], cc_rsem.at[other], partner
        ).wait_recv()
    own_copy(0).wait()
    dw_ref[...] = dot(
        att_all[...].reshape(group * rows, width), cot_cols[...].reshape(group * rows, half), TN
    )

    stores[4].start()

    @pl.when(b == 0)
    def _():
        dkv_copy().wait_recv()
        dk_ref[0] = (dkv_own[0] + dkv_recv[0].astype(jnp.float32)).astype(jnp.bfloat16)
        dv_ref[0] = (dkv_own[1] + dkv_recv[1].astype(jnp.float32)).astype(jnp.bfloat16)

    stores[2].start()
    stores[3].start()

    for c in range(chunks):
        mine = partial(m, c)
        at = slice(c * part, (c + 1) * part)

        @pl.when(m > 0)
        def _():
            sum_up(m, c).wait_recv()

        @pl.when(m < nm - 1)
        def _():
            sum_down(m, c).wait_recv()

        @pl.when(m == 0)
        def _():
            mixed_ref[0, :, at] = (mine + down_in[m, c].astype(jnp.float32)).astype(jnp.bfloat16)

        @pl.when(m == nm - 1)
        def _():
            mixed_ref[0, :, at] = (mine + up_in[m, c].astype(jnp.float32)).astype(jnp.bfloat16)

        @pl.when(jnp.logical_and(m > 0, m < nm - 1))
        def _():
            mixed_ref[0, :, at] = (
                mine + up_in[m, c].astype(jnp.float32) + down_in[m, c].astype(jnp.float32)
            ).astype(jnp.bfloat16)

    stores[0].start()

    for shard in range(nm):
        @pl.when(jnp.logical_and(m < nm - 1, shard <= m))
        def _():
            gather_up(shard).wait_send()

        @pl.when(jnp.logical_and(m > 0, shard >= m))
        def _():
            gather_down(shard).wait_send()

        for to_b in range(nb):
            @pl.when(jnp.logical_not(jnp.logical_and(shard == d, b == to_b)))
            def _():
                column_copy(shard, to_b).wait_send()

        for c in range(chunks):
            @pl.when(shard > m)
            def _():
                sum_up(shard, c).wait_send()

            @pl.when(shard < m)
            def _():
                sum_down(shard, c).wait_send()

    for off in range(1, pairs):
        att_copy(off).wait_send()
    for off in range(pairs):
        att_pass(off).wait_send()

    @pl.when(b == 0)
    def _():
        for copy in kv_copies():
            copy.wait_send()

    @pl.when(b == 1)
    def _():
        dkv_copy().wait_send()

    for copy in stores:
        copy.wait()


def write_kernel(*refs):
    sources, results, held = refs[:5], refs[5:10], refs[10:15]
    in_sem, out_sem = refs[15:]
    reads = [pltpu.make_async_copy(sources[i], held[i], in_sem.at[i]) for i in range(5)]
    writes = [pltpu.make_async_copy(held[i], results[i], out_sem.at[i]) for i in range(5)]
    for copy in reads:
        copy.start()
    for read, write in zip(reads, writes):
        read.wait()
        write.start()
    for copy in writes:
        copy.wait()


def fused(nd, nm, queries, keys, values, clip_ids, w_out, cotangent):
    nb, chunks = 2, 2
    group = nd * nb
    _, rows, width = queries.shape
    piece = cotangent.shape[2]
    half, part = piece // nb, piece // chunks
    heads = width // HD
    lanes = -(-rows // 128) * 128
    bf16, f32 = jnp.bfloat16, jnp.float32
    dma = pltpu.SemaphoreType.DMA
    results = pl.pallas_call(
        functools.partial(fused_kernel, nd, nm, chunks),
        out_shape=(
            jax.ShapeDtypeStruct((1, rows, piece), bf16),
            jax.ShapeDtypeStruct((1, rows, width), bf16),
            jax.ShapeDtypeStruct((1, rows, width), bf16),
            jax.ShapeDtypeStruct((1, rows, width), bf16),
            jax.ShapeDtypeStruct((width, half), f32),
        ),
        in_specs=[pl.BlockSpec(memory_space=pltpu.HBM)] * 6,
        out_specs=(pl.BlockSpec(memory_space=pltpu.HBM),) * 5,
        scratch_shapes=[
            pltpu.VMEM((1, rows, piece), bf16),
            pltpu.VMEM((1, rows, width), bf16),
            pltpu.VMEM((1, rows, width), bf16),
            pltpu.VMEM((1, rows, width), bf16),
            pltpu.VMEM((width, half), f32),
            dma((5,)),
            pltpu.VMEM(queries.shape, bf16),
            pltpu.VMEM(queries.shape, bf16),
            pltpu.VMEM(queries.shape, bf16),
            pltpu.VMEM(clip_ids.shape, jnp.int32),
            pltpu.VMEM(w_out.shape, bf16),
            pltpu.VMEM((nm, rows, piece), bf16),
            pltpu.VMEM((group, rows, half), bf16),
            pltpu.VMEM((group, rows, width), bf16),
            pltpu.VMEM((2, rows, width), bf16),
            pltpu.VMEM((8, lanes), jnp.int32),
            pltpu.VMEM((8, lanes), jnp.int32),
            pltpu.VMEM((heads, rows, rows), f32),
            pltpu.VMEM((heads, rows, rows), f32),
            pltpu.VMEM((rows, width), bf16),
            pltpu.VMEM((2, rows, width), f32),
            pltpu.VMEM((2, rows, width), bf16),
            pltpu.VMEM((2, rows, width), bf16),
            pltpu.VMEM((nm, chunks, rows, part), bf16),
            pltpu.VMEM((nm, chunks, rows, part), bf16),
            pltpu.VMEM((nm, chunks, rows, part), bf16),
            pltpu.VMEM((nm, chunks, rows, part), bf16),
            dma((5,)), dma, dma, dma((3,)), dma((3,)), dma((nm,)), dma((nm,)), dma((nm,)),
            dma((nm, nb)), dma((group,)), dma((group,)), dma((group,)),
            dma((nm, chunks)), dma((nm, chunks)), dma((nm, chunks)), dma((nm, chunks)), dma, dma,
        ],
        compiler_params=pltpu.CompilerParams(
            collective_id=0, has_side_effects=True, vmem_limit_bytes=61 * 1024 * 1024
        ),
    )(queries, keys, values, clip_ids, w_out, cotangent)
    return pl.pallas_call(
        write_kernel,
        out_shape=tuple(jax.ShapeDtypeStruct(x.shape, x.dtype) for x in results),
        in_specs=[pl.BlockSpec(memory_space=pltpu.HBM)] * 5,
        out_specs=(pl.BlockSpec(memory_space=pltpu.HBM),) * 5,
        scratch_shapes=[pltpu.VMEM(x.shape, x.dtype) for x in results] + [dma((5,)), dma((5,))],
        compiler_params=pltpu.CompilerParams(vmem_limit_bytes=61 * 1024 * 1024),
    )(*results)


def seen_mask(q_pos, q_clip, k_pos, k_clip):
    return (k_pos[None, :] <= q_pos[:, None]) & (k_clip[None, :] == q_clip[:, None])


def per_device(queries, keys, values, clip_ids, w_out, cotangent):
    q_here = queries[0]
    k_here = keys[0]
    v_here = values[0]
    rows = q_here.shape[0]
    width = q_here.shape[1]
    heads = width // HD
    scale = HD ** (-0.5)
    first = lax.axis_index("blk") * rows
    q_pos = first + jnp.arange(rows, dtype=jnp.int32)
    clips_all = lax.all_gather(clip_ids[0], "blk", axis=0, tiled=True)
    clip_here = lax.dynamic_slice_in_dim(clips_all, first, rows, 0)
    qh = q_here.reshape(rows, heads, HD)
    kh = k_here.reshape(rows, heads, HD)
    vh = v_here.reshape(rows, heads, HD)
    k_piece = lax.all_gather(k_here, "blk", axis=0, tiled=True)
    v_piece = lax.all_gather(v_here, "blk", axis=0, tiled=True)
    count = k_piece.shape[0]
    k_pos = jnp.arange(count, dtype=jnp.int32)
    k_clip = clips_all
    allowed = seen_mask(q_pos, clip_here, k_pos, k_clip)
    peak = jnp.full((heads, rows), NEG, jnp.float32)
    accum = jnp.zeros((rows, heads, HD), jnp.float32)
    scores = (
        jnp.einsum(
            "qhd,khd->hqk",
            qh,
            k_piece.reshape(count, heads, HD),
            preferred_element_type=jnp.float32,
        )
        * scale
    )
    scores = jnp.where(allowed[None], scores, NEG)
    new_peak = jnp.maximum(peak, jnp.max(scores, axis=-1))
    factor = jnp.exp(peak - new_peak)
    probs = jnp.where(allowed[None], jnp.exp(scores - new_peak[:, :, None]), 0.0)
    total = jnp.sum(probs, axis=-1)
    v_block = v_piece.reshape(count, heads, HD).astype(jnp.float32)
    accum = accum * factor.T[:, :, None] + jnp.einsum(
        "hqk,khd->qhd",
        probs,
        v_block,
        precision=lax.Precision.HIGHEST,
        preferred_element_type=jnp.float32,
    )
    peak, total, accum = (new_peak, total, accum)
    lse = peak + jnp.log(total)
    attended = (accum / total.T[:, :, None]).astype(jnp.bfloat16).reshape(rows, width)
    partial_value = jnp.dot(attended, w_out, preferred_element_type=jnp.float32)
    mixed = lax.psum_scatter(partial_value, "mp", scatter_dimension=1, tiled=True).astype(
        jnp.bfloat16
    )
    cot_full = lax.all_gather(cotangent[0], "mp", axis=1, tiled=True)
    d_att = lax.dot_general(
        cot_full, w_out, (((1,), (1,)), ((), ())), preferred_element_type=jnp.float32
    ).astype(jnp.bfloat16)
    doh = d_att.reshape(rows, heads, HD)
    delta = jnp.sum(
        doh.astype(jnp.float32) * attended.reshape(rows, heads, HD).astype(jnp.float32), axis=-1
    )
    lse_all, delta_all = (
        lax.all_gather(lse.T, "blk", axis=0, tiled=True),
        lax.all_gather(delta, "blk", axis=0, tiled=True),
    )
    k_piece = lax.all_gather(k_here, "blk", axis=0, tiled=True)
    v_piece = lax.all_gather(v_here, "blk", axis=0, tiled=True)
    count = k_piece.shape[0]
    k_pos = jnp.arange(count, dtype=jnp.int32)
    k_clip = clips_all
    allowed = seen_mask(q_pos, clip_here, k_pos, k_clip)
    k_heads = k_piece.reshape(count, heads, HD)
    scores = jnp.einsum("qhd,khd->hqk", qh, k_heads, preferred_element_type=jnp.float32) * scale
    probs = jnp.where(
        allowed[None], jnp.exp(jnp.where(allowed[None], scores, NEG) - lse[:, :, None]), 0.0
    )
    d_probs = jnp.einsum(
        "qhd,khd->hqk", doh, v_piece.reshape(count, heads, HD), preferred_element_type=jnp.float32
    )
    d_scores = (probs * (d_probs - delta.T[:, :, None])).astype(jnp.bfloat16)
    dq_sum = jnp.einsum("hqk,khd->qhd", d_scores, k_heads, preferred_element_type=jnp.float32)
    q_piece = lax.all_gather(q_here, "blk", axis=0, tiled=True)
    do_piece = lax.all_gather(d_att, "blk", axis=0, tiled=True)
    count = q_piece.shape[0]
    p_pos = jnp.arange(count, dtype=jnp.int32)
    allowed = seen_mask(p_pos, clips_all, q_pos, clip_here)
    q_heads = q_piece.reshape(count, heads, HD)
    do_heads = do_piece.reshape(count, heads, HD)
    scores = jnp.einsum("qhd,khd->hqk", q_heads, kh, preferred_element_type=jnp.float32) * scale
    probs = jnp.where(
        allowed[None], jnp.exp(jnp.where(allowed[None], scores, NEG) - lse_all.T[:, :, None]), 0.0
    )
    dv_acc = jnp.einsum(
        "hqk,qhd->khd", probs.astype(jnp.bfloat16), do_heads, preferred_element_type=jnp.float32
    )
    d_probs = jnp.einsum("qhd,khd->hqk", do_heads, vh, preferred_element_type=jnp.float32)
    d_scores = (probs * (d_probs - delta_all.T[:, :, None])).astype(jnp.bfloat16)
    dk_acc = jnp.einsum("hqk,qhd->khd", d_scores, q_heads, preferred_element_type=jnp.float32)
    d_queries = (dq_sum * scale).astype(jnp.bfloat16).reshape(1, rows, width)
    d_keys = (dk_acc * scale).astype(jnp.bfloat16).reshape(1, rows, width)
    d_values = dv_acc.astype(jnp.bfloat16).reshape(1, rows, width)
    local_grad = lax.dot_general(
        attended, cot_full, (((0,), (0,)), ((), ())), preferred_element_type=jnp.float32
    )
    d_w_out = lax.psum_scatter(local_grad, ("dp", "blk"), scatter_dimension=1, tiled=True)
    return (mixed[None], d_queries, d_keys, d_values, d_w_out)


def solution(mesh):
    placed = (
        P("dp", "blk", "mp"),
        P("dp", "blk", "mp"),
        P("dp", "blk", "mp"),
        P("dp", "blk"),
        P("mp", None),
        P("dp", "blk", "mp"),
    )
    nd, nb, nm = mesh.shape["dp"], mesh.shape["blk"], mesh.shape["mp"]
    body = per_device
    if nb == 2 and nd == nm and nd % 2 == 0:
        body = functools.partial(fused, nd, nm)
    return jax.shard_map(
        body,
        mesh=mesh,
        in_specs=placed,
        out_specs=(
            P("dp", "blk", "mp"),
            P("dp", "blk", "mp"),
            P("dp", "blk", "mp"),
            P("dp", "blk", "mp"),
            P("mp", ("dp", "blk")),
        ),
        check_vma=False,
    )
```

```python
import functools

import jax
import jax.numpy as jnp
from jax import lax
from jax.experimental import pallas as pl
from jax.experimental.pallas import tpu as pltpu
from jax.sharding import PartitionSpec as P

HD = 128
NEG = -1e30
MESH = pl.DeviceIdType.MESH
NN = (((1,), (0,)), ((), ()))
NT = (((1,), (1,)), ((), ()))
TN = (((0,), (0,)), ((), ()))


def dot(a, b, dims):
    return lax.dot_general(a, b, dims, preferred_element_type=jnp.float32)


def fused_kernel(
    nd, nm, chunks,
    q_hbm, k_hbm, v_hbm, clip_hbm, w_hbm, cot_hbm,
    mixed_hbm, dq_hbm, dk_hbm, dv_hbm, dw_hbm,
    mixed_ref, dq_ref, dk_ref, dv_ref, dw_ref, out_sem,
    q_ref, k_ref, v_ref, clip_ref, w_ref, cot_full, cot_cols, att_all, kv_prev, clip_send, clip_prev,
    p_own, p_prev, d_att, dkv_own, dkv_send, dkv_recv,
    up_out, up_in, down_out, down_in,
    in_sem, w_sem, own_sem, kv_ssem, kv_rsem, ag_up_ssem, ag_dn_ssem, ag_rsem,
    cc_ssem, cc_rsem, at_ssem, at_rsem,
    up_ssem, up_rsem, dn_ssem, dn_rsem, dkv_ssem, dkv_rsem,
):
    nb = 2
    d, b, m = lax.axis_index("dp"), lax.axis_index("blk"), lax.axis_index("mp")
    me = d * nb + b
    group = nd * nb
    rows, width = q_ref.shape[1], q_ref.shape[2]
    heads = width // HD
    scale = HD ** (-0.5)
    piece = cot_full.shape[2]
    half = piece // nb
    part = piece // chunks

    def remote(src, dst, ssem, rsem, device):
        return pltpu.make_async_remote_copy(
            src_ref=src, dst_ref=dst, send_sem=ssem, recv_sem=rsem,
            device_id=device, device_id_type=MESH,
        )

    w_copy = pltpu.make_async_copy(w_hbm, w_ref, w_sem)
    fetches = [
        pltpu.make_async_copy(src, dst, in_sem.at[i])
        for i, (src, dst) in enumerate((
            (cot_hbm.at[0], cot_full.at[m]), (k_hbm, k_ref), (v_hbm, v_ref), (q_hbm, q_ref),
            (clip_hbm, clip_ref),
        ))
    ]
    for copy in fetches:
        copy.start()
    w_copy.start()

    barrier = pltpu.get_barrier_semaphore()
    for off in range(1, group):
        other = lax.rem(me + off, group)
        pl.semaphore_signal(
            barrier, inc=1, device_id=(other // nb, lax.rem(other, nb), m), device_id_type=MESH
        )

    @pl.when(m > 0)
    def _():
        pl.semaphore_signal(barrier, inc=1, device_id=(d, b, m - 1), device_id_type=MESH)

    @pl.when(m < nm - 1)
    def _():
        pl.semaphore_signal(barrier, inc=1, device_id=(d, b, m + 1), device_id_type=MESH)

    clip_send[...] = jnp.zeros_like(clip_send)
    for copy in fetches:
        copy.wait()
    clip_send[0:1, 0:rows] = clip_ref[...]
    pl.semaphore_wait(
        barrier, group - 1 + jnp.where(m > 0, 1, 0) + jnp.where(m < nm - 1, 1, 0)
    )

    def kv_copies():
        peer = (d, 1, m)
        return (
            remote(k_ref.at[0], kv_prev.at[0], kv_ssem.at[0], kv_rsem.at[0], peer),
            remote(v_ref.at[0], kv_prev.at[1], kv_ssem.at[1], kv_rsem.at[1], peer),
            remote(clip_send, clip_prev, kv_ssem.at[2], kv_rsem.at[2], peer),
        )

    def gather_up(shard):
        return remote(
            cot_full.at[shard], cot_full.at[shard], ag_up_ssem.at[shard], ag_rsem.at[shard],
            (d, b, m + 1),
        )

    def gather_down(shard):
        return remote(
            cot_full.at[shard], cot_full.at[shard], ag_dn_ssem.at[shard], ag_rsem.at[shard],
            (d, b, m - 1),
        )

    def column_copy(shard, to_b):
        return remote(
            cot_full.at[shard, :, pl.ds(to_b * half, half)], cot_cols.at[me],
            cc_ssem.at[shard, to_b], cc_rsem.at[me], (shard, to_b, m),
        )

    def own_copy(to_b):
        return pltpu.make_async_copy(
            cot_full.at[d, :, pl.ds(to_b * half, half)], cot_cols.at[me], own_sem
        )

    def each_column(shard, away, here):
        for to_b in range(nb):
            is_me = jnp.logical_and(shard == d, b == to_b)

            @pl.when(jnp.logical_not(is_me))
            def _():
                away(column_copy(shard, to_b))

            @pl.when(is_me)
            def _():
                here(own_copy(to_b))

    def start(copy):
        copy.start()

    @pl.when(m < nm - 1)
    def _():
        gather_up(m).start()

    @pl.when(m > 0)
    def _():
        gather_down(m).start()

    @pl.when(b == 0)
    def _():
        for copy in kv_copies():
            copy.start()

    @pl.when(b == 1)
    def _():
        each_column(m, start, start)

    def gather_step(step):
        @pl.when(m - step >= 0)
        def _():
            shard = m - step
            gather_down(shard).wait_recv()

            @pl.when(m < nm - 1)
            def _():
                gather_up(shard).start()

            each_column(shard, start, start)

        @pl.when(m + step < nm)
        def _():
            shard = m + step
            gather_up(shard).wait_recv()

            @pl.when(m > 0)
            def _():
                gather_down(shard).start()

            each_column(shard, start, start)

    row = lax.broadcasted_iota(jnp.int32, (rows, rows), 0)
    col = lax.broadcasted_iota(jnp.int32, (rows, rows), 1)

    def clip_rows(ref):
        return jnp.broadcast_to(ref[0:1, 0:rows], (rows, rows))

    def own_scores(h):
        cols = pl.ds(h * HD, HD)
        return jnp.where(seen, dot(q_ref[0, :, cols], k_ref[0, :, cols], NT) * scale, NEG)

    here = clip_rows(clip_send)
    mine = jnp.sum(jnp.where(row == col, here, 0), axis=1, keepdims=True)
    seen = jnp.logical_and(col <= row, here == mine)

    @pl.when(b == 0)
    def _():
        for h in range(heads):
            cols = pl.ds(h * HD, HD)
            s = own_scores(h)
            e = jnp.exp(s - jnp.max(s, axis=1, keepdims=True))
            e = e * (1.0 / jnp.sum(e, axis=1, keepdims=True))
            p_own[h] = e
            att = dot(e.astype(jnp.bfloat16), v_ref[0, :, cols], NN)
            att_all[me, :, cols] = att.astype(jnp.bfloat16)

    @pl.when(b == 1)
    def _():
        for h in range(heads):
            p_own[h] = own_scores(h)

    gather_step(1)

    @pl.when(b == 0)
    def _():
        each_column(m, start, start)

    @pl.when(b == 1)
    def _():
        k_copy, v_copy, clip_copy = kv_copies()
        clip_copy.wait_recv()
        k_copy.wait_recv()
        earlier = clip_rows(clip_prev) == mine
        for h in range(heads):
            cols = pl.ds(h * HD, HD)
            s = p_own[h]
            t = jnp.where(
                earlier, dot(q_ref[0, :, cols], kv_prev[0, :, cols], NT) * scale, NEG
            )
            peak = jnp.maximum(
                jnp.max(s, axis=1, keepdims=True), jnp.max(t, axis=1, keepdims=True)
            )
            e, f = jnp.exp(s - peak), jnp.exp(t - peak)
            inverse = 1.0 / (
                jnp.sum(e, axis=1, keepdims=True) + jnp.sum(f, axis=1, keepdims=True)
            )
            e, f = e * inverse, f * inverse
            p_own[h] = e
            p_prev[h] = f
            dkv_own[0, :, cols] = dot(e.astype(jnp.bfloat16), v_ref[0, :, cols], NN)
        v_copy.wait_recv()
        for h in range(heads):
            cols = pl.ds(h * HD, HD)
            att = dkv_own[0, :, cols] + dot(
                p_prev[h].astype(jnp.bfloat16), kv_prev[1, :, cols], NN
            )
            att_all[me, :, cols] = att.astype(jnp.bfloat16)

    pairs = group // 2
    core = lax.rem(d, 2)
    partner = (d + 1 - 2 * core, b, m)
    pair = (d // 2) * nb + b

    def att_slot(off):
        other = lax.rem(pair + off, pairs)
        return (other // nb) * 2 + core, lax.rem(other, nb)

    def att_copy(off):
        to_d, to_b = att_slot(off)
        return remote(
            att_all.at[me], att_all.at[me], at_ssem.at[off], at_rsem.at[me], (to_d, to_b, m)
        )

    def att_pass(off):
        of_d, of_b = att_slot(off)
        slot = of_d * nb + of_b
        return remote(
            att_all.at[slot], att_all.at[slot], at_ssem.at[pairs + off], at_rsem.at[slot], partner
        )

    for off in range(1, pairs):
        att_copy(off).start()
    att_pass(0).start()

    w_copy.wait()

    def partial(dest, c):
        at = pl.multiple_of(dest * piece + c * part, part)
        return dot(att_all[me], w_ref[:, pl.ds(at, part)], NN)

    def sum_up(dest, c):
        return remote(
            up_out.at[dest, c], up_in.at[dest, c], up_ssem.at[dest, c], up_rsem.at[dest, c],
            (d, b, m + 1),
        )

    def sum_down(dest, c):
        return remote(
            down_out.at[dest, c], down_in.at[dest, c], dn_ssem.at[dest, c], dn_rsem.at[dest, c],
            (d, b, m - 1),
        )

    def chain_step(step):
        for c in range(chunks):
            @pl.when(step >= m)
            def _():
                dest = nm - 1 - step + m
                mine = partial(dest, c)

                @pl.when(m == 0)
                def _():
                    up_out[dest, c] = mine.astype(jnp.bfloat16)

                @pl.when(m > 0)
                def _():
                    sum_up(dest, c).wait_recv()
                    up_out[dest, c] = (
                        mine + up_in[dest, c].astype(jnp.float32)
                    ).astype(jnp.bfloat16)

                sum_up(dest, c).start()

            @pl.when(step >= nm - 1 - m)
            def _():
                dest = step - (nm - 1 - m)
                mine = partial(dest, c)

                @pl.when(m == nm - 1)
                def _():
                    down_out[dest, c] = mine.astype(jnp.bfloat16)

                @pl.when(m < nm - 1)
                def _():
                    sum_down(dest, c).wait_recv()
                    down_out[dest, c] = (
                        mine + down_in[dest, c].astype(jnp.float32)
                    ).astype(jnp.bfloat16)

                sum_down(dest, c).start()

    at_end = jnp.logical_or(m == 0, m == nm - 1)
    for step in range(nm - 2):
        chain_step(step)
        if step == nm - 3:
            @pl.when(at_end)
            def _():
                chain_step(nm - 2)

        gather_step(step + 2)

    total = dot(cot_full[0], w_ref[:, 0:piece], NT)
    for shard in range(1, nm):
        total = total + dot(cot_full[shard], w_ref[:, shard * piece:(shard + 1) * piece], NT)
    d_att[...] = total.astype(jnp.bfloat16)

    def dkv_copy():
        return remote(dkv_send, dkv_recv, dkv_ssem, dkv_rsem, (d, 0, m))

    def backward(use_prev):
        for h in range(heads):
            cols = pl.ds(h * HD, HD)
            do = d_att[:, cols]
            q = q_ref[0, :, cols]
            delta = jnp.sum(
                do.astype(jnp.float32) * att_all[me, :, cols].astype(jnp.float32),
                axis=1, keepdims=True,
            )
            e = p_own[h]
            ds = (e * (dot(do, v_ref[0, :, cols], NT) - delta)).astype(jnp.bfloat16)
            dq = dot(ds, k_ref[0, :, cols], NN)
            dk = dot(ds, q, TN) * scale
            dv = dot(e.astype(jnp.bfloat16), do, TN)
            if use_prev:
                f = p_prev[h]
                dt = (f * (dot(do, kv_prev[1, :, cols], NT) - delta)).astype(jnp.bfloat16)
                dq = dq + dot(dt, kv_prev[0, :, cols], NN)
                dkv_send[0, :, cols] = (dot(dt, q, TN) * scale).astype(jnp.bfloat16)
                dkv_send[1, :, cols] = dot(f.astype(jnp.bfloat16), do, TN).astype(jnp.bfloat16)
                dk_ref[0, :, cols] = dk.astype(jnp.bfloat16)
                dv_ref[0, :, cols] = dv.astype(jnp.bfloat16)
            else:
                dkv_own[0, :, cols] = dk
                dkv_own[1, :, cols] = dv
            dq_ref[0, :, cols] = (dq * scale).astype(jnp.bfloat16)

    @pl.when(b == 0)
    def _():
        backward(False)

    @pl.when(b == 1)
    def _():
        backward(True)
        dkv_copy().start()

    stores = [
        pltpu.make_async_copy(src, dst, out_sem.at[i])
        for i, (src, dst) in enumerate((
            (mixed_ref, mixed_hbm), (dq_ref, dq_hbm), (dk_ref, dk_hbm), (dv_ref, dv_hbm),
            (dw_ref, dw_hbm),
        ))
    ]
    stores[1].start()

    for off in range(1, pairs):
        att_pass(off).wait_recv()
        att_pass(off).start()

    @pl.when(jnp.logical_not(at_end))
    def _():
        chain_step(nm - 2)

    for off in range(pairs):
        of_d, of_b = att_slot(off)
        slot = (of_d + 1 - 2 * core) * nb + of_b
        remote(
            att_all.at[slot], att_all.at[slot], at_ssem.at[0], at_rsem.at[slot], partner
        ).wait_recv()
    for off in range(1, group):
        other = lax.rem(me + off, group)
        remote(
            cot_cols.at[other], cot_cols.at[other], cc_ssem.at[0, 0], cc_rsem.at[other], partner
        ).wait_recv()
    own_copy(0).wait()
    dw_ref[...] = dot(
        att_all[...].reshape(group * rows, width), cot_cols[...].reshape(group * rows, half), TN
    )

    stores[4].start()

    @pl.when(b == 0)
    def _():
        dkv_copy().wait_recv()
        dk_ref[0] = (dkv_own[0] + dkv_recv[0].astype(jnp.float32)).astype(jnp.bfloat16)
        dv_ref[0] = (dkv_own[1] + dkv_recv[1].astype(jnp.float32)).astype(jnp.bfloat16)

    stores[2].start()
    stores[3].start()

    for c in range(chunks):
        mine = partial(m, c)
        at = slice(c * part, (c + 1) * part)

        @pl.when(m > 0)
        def _():
            sum_up(m, c).wait_recv()

        @pl.when(m < nm - 1)
        def _():
            sum_down(m, c).wait_recv()

        @pl.when(m == 0)
        def _():
            mixed_ref[0, :, at] = (mine + down_in[m, c].astype(jnp.float32)).astype(jnp.bfloat16)

        @pl.when(m == nm - 1)
        def _():
            mixed_ref[0, :, at] = (mine + up_in[m, c].astype(jnp.float32)).astype(jnp.bfloat16)

        @pl.when(jnp.logical_and(m > 0, m < nm - 1))
        def _():
            mixed_ref[0, :, at] = (
                mine + up_in[m, c].astype(jnp.float32) + down_in[m, c].astype(jnp.float32)
            ).astype(jnp.bfloat16)

    stores[0].start()

    for shard in range(nm):
        @pl.when(jnp.logical_and(m < nm - 1, shard <= m))
        def _():
            gather_up(shard).wait_send()

        @pl.when(jnp.logical_and(m > 0, shard >= m))
        def _():
            gather_down(shard).wait_send()

        for to_b in range(nb):
            @pl.when(jnp.logical_not(jnp.logical_and(shard == d, b == to_b)))
            def _():
                column_copy(shard, to_b).wait_send()

        for c in range(chunks):
            @pl.when(shard > m)
            def _():
                sum_up(shard, c).wait_send()

            @pl.when(shard < m)
            def _():
                sum_down(shard, c).wait_send()

    for off in range(1, pairs):
        att_copy(off).wait_send()
    for off in range(pairs):
        att_pass(off).wait_send()

    @pl.when(b == 0)
    def _():
        for copy in kv_copies():
            copy.wait_send()

    @pl.when(b == 1)
    def _():
        dkv_copy().wait_send()

    for copy in stores:
        copy.wait()


def write_kernel(*refs):
    sources, results, held = refs[:5], refs[5:10], refs[10:15]
    in_sem, out_sem = refs[15:]
    reads = [pltpu.make_async_copy(sources[i], held[i], in_sem.at[i]) for i in range(5)]
    writes = [pltpu.make_async_copy(held[i], results[i], out_sem.at[i]) for i in range(5)]
    for copy in reads:
        copy.start()
    for read, write in zip(reads, writes):
        read.wait()
        write.start()
    for copy in writes:
        copy.wait()


def fused(nd, nm, queries, keys, values, clip_ids, w_out, cotangent):
    nb, chunks = 2, 2
    group = nd * nb
    _, rows, width = queries.shape
    piece = cotangent.shape[2]
    half, part = piece // nb, piece // chunks
    heads = width // HD
    lanes = -(-rows // 128) * 128
    bf16, f32 = jnp.bfloat16, jnp.float32
    dma = pltpu.SemaphoreType.DMA
    results = pl.pallas_call(
        functools.partial(fused_kernel, nd, nm, chunks),
        out_shape=(
            jax.ShapeDtypeStruct((1, rows, piece), bf16),
            jax.ShapeDtypeStruct((1, rows, width), bf16),
            jax.ShapeDtypeStruct((1, rows, width), bf16),
            jax.ShapeDtypeStruct((1, rows, width), bf16),
            jax.ShapeDtypeStruct((width, half), f32),
        ),
        in_specs=[pl.BlockSpec(memory_space=pltpu.HBM)] * 6,
        out_specs=(pl.BlockSpec(memory_space=pltpu.HBM),) * 5,
        scratch_shapes=[
            pltpu.VMEM((1, rows, piece), bf16),
            pltpu.VMEM((1, rows, width), bf16),
            pltpu.VMEM((1, rows, width), bf16),
            pltpu.VMEM((1, rows, width), bf16),
            pltpu.VMEM((width, half), f32),
            dma((5,)),
            pltpu.VMEM(queries.shape, bf16),
            pltpu.VMEM(queries.shape, bf16),
            pltpu.VMEM(queries.shape, bf16),
            pltpu.VMEM(clip_ids.shape, jnp.int32),
            pltpu.VMEM(w_out.shape, bf16),
            pltpu.VMEM((nm, rows, piece), bf16),
            pltpu.VMEM((group, rows, half), bf16),
            pltpu.VMEM((group, rows, width), bf16),
            pltpu.VMEM((2, rows, width), bf16),
            pltpu.VMEM((8, lanes), jnp.int32),
            pltpu.VMEM((8, lanes), jnp.int32),
            pltpu.VMEM((heads, rows, rows), f32),
            pltpu.VMEM((heads, rows, rows), f32),
            pltpu.VMEM((rows, width), bf16),
            pltpu.VMEM((2, rows, width), f32),
            pltpu.VMEM((2, rows, width), bf16),
            pltpu.VMEM((2, rows, width), bf16),
            pltpu.VMEM((nm, chunks, rows, part), bf16),
            pltpu.VMEM((nm, chunks, rows, part), bf16),
            pltpu.VMEM((nm, chunks, rows, part), bf16),
            pltpu.VMEM((nm, chunks, rows, part), bf16),
            dma((5,)), dma, dma, dma((3,)), dma((3,)), dma((nm,)), dma((nm,)), dma((nm,)),
            dma((nm, nb)), dma((group,)), dma((group,)), dma((group,)),
            dma((nm, chunks)), dma((nm, chunks)), dma((nm, chunks)), dma((nm, chunks)), dma, dma,
        ],
        compiler_params=pltpu.CompilerParams(
            collective_id=0, has_side_effects=True, vmem_limit_bytes=61 * 1024 * 1024
        ),
    )(queries, keys, values, clip_ids, w_out, cotangent)
    return pl.pallas_call(
        write_kernel,
        out_shape=tuple(jax.ShapeDtypeStruct(x.shape, x.dtype) for x in results),
        in_specs=[pl.BlockSpec(memory_space=pltpu.HBM)] * 5,
        out_specs=(pl.BlockSpec(memory_space=pltpu.HBM),) * 5,
        scratch_shapes=[pltpu.VMEM(x.shape, x.dtype) for x in results] + [dma((5,)), dma((5,))],
        compiler_params=pltpu.CompilerParams(vmem_limit_bytes=61 * 1024 * 1024),
    )(*results)


def seen_mask(q_pos, q_clip, k_pos, k_clip):
    return (k_pos[None, :] <= q_pos[:, None]) & (k_clip[None, :] == q_clip[:, None])


def per_device(queries, keys, values, clip_ids, w_out, cotangent):
    q_here = queries[0]
    k_here = keys[0]
    v_here = values[0]
    rows = q_here.shape[0]
    width = q_here.shape[1]
    heads = width // HD
    scale = HD ** (-0.5)
    first = lax.axis_index("blk") * rows
    q_pos = first + jnp.arange(rows, dtype=jnp.int32)
    clips_all = lax.all_gather(clip_ids[0], "blk", axis=0, tiled=True)
    clip_here = lax.dynamic_slice_in_dim(clips_all, first, rows, 0)
    qh = q_here.reshape(rows, heads, HD)
    kh = k_here.reshape(rows, heads, HD)
    vh = v_here.reshape(rows, heads, HD)
    k_piece = lax.all_gather(k_here, "blk", axis=0, tiled=True)
    v_piece = lax.all_gather(v_here, "blk", axis=0, tiled=True)
    count = k_piece.shape[0]
    k_pos = jnp.arange(count, dtype=jnp.int32)
    k_clip = clips_all
    allowed = seen_mask(q_pos, clip_here, k_pos, k_clip)
    peak = jnp.full((heads, rows), NEG, jnp.float32)
    accum = jnp.zeros((rows, heads, HD), jnp.float32)
    scores = (
        jnp.einsum(
            "qhd,khd->hqk",
            qh,
            k_piece.reshape(count, heads, HD),
            preferred_element_type=jnp.float32,
        )
        * scale
    )
    scores = jnp.where(allowed[None], scores, NEG)
    new_peak = jnp.maximum(peak, jnp.max(scores, axis=-1))
    factor = jnp.exp(peak - new_peak)
    probs = jnp.where(allowed[None], jnp.exp(scores - new_peak[:, :, None]), 0.0)
    total = jnp.sum(probs, axis=-1)
    v_block = v_piece.reshape(count, heads, HD).astype(jnp.float32)
    accum = accum * factor.T[:, :, None] + jnp.einsum(
        "hqk,khd->qhd",
        probs,
        v_block,
        precision=lax.Precision.HIGHEST,
        preferred_element_type=jnp.float32,
    )
    peak, total, accum = (new_peak, total, accum)
    lse = peak + jnp.log(total)
    attended = (accum / total.T[:, :, None]).astype(jnp.bfloat16).reshape(rows, width)
    partial_value = jnp.dot(attended, w_out, preferred_element_type=jnp.float32)
    mixed = lax.psum_scatter(partial_value, "mp", scatter_dimension=1, tiled=True).astype(
        jnp.bfloat16
    )
    cot_full = lax.all_gather(cotangent[0], "mp", axis=1, tiled=True)
    d_att = lax.dot_general(
        cot_full, w_out, (((1,), (1,)), ((), ())), preferred_element_type=jnp.float32
    ).astype(jnp.bfloat16)
    doh = d_att.reshape(rows, heads, HD)
    delta = jnp.sum(
        doh.astype(jnp.float32) * attended.reshape(rows, heads, HD).astype(jnp.float32), axis=-1
    )
    lse_all, delta_all = (
        lax.all_gather(lse.T, "blk", axis=0, tiled=True),
        lax.all_gather(delta, "blk", axis=0, tiled=True),
    )
    k_piece = lax.all_gather(k_here, "blk", axis=0, tiled=True)
    v_piece = lax.all_gather(v_here, "blk", axis=0, tiled=True)
    count = k_piece.shape[0]
    k_pos = jnp.arange(count, dtype=jnp.int32)
    k_clip = clips_all
    allowed = seen_mask(q_pos, clip_here, k_pos, k_clip)
    k_heads = k_piece.reshape(count, heads, HD)
    scores = jnp.einsum("qhd,khd->hqk", qh, k_heads, preferred_element_type=jnp.float32) * scale
    probs = jnp.where(
        allowed[None], jnp.exp(jnp.where(allowed[None], scores, NEG) - lse[:, :, None]), 0.0
    )
    d_probs = jnp.einsum(
        "qhd,khd->hqk", doh, v_piece.reshape(count, heads, HD), preferred_element_type=jnp.float32
    )
    d_scores = (probs * (d_probs - delta.T[:, :, None])).astype(jnp.bfloat16)
    dq_sum = jnp.einsum("hqk,khd->qhd", d_scores, k_heads, preferred_element_type=jnp.float32)
    q_piece = lax.all_gather(q_here, "blk", axis=0, tiled=True)
    do_piece = lax.all_gather(d_att, "blk", axis=0, tiled=True)
    count = q_piece.shape[0]
    p_pos = jnp.arange(count, dtype=jnp.int32)
    allowed = seen_mask(p_pos, clips_all, q_pos, clip_here)
    q_heads = q_piece.reshape(count, heads, HD)
    do_heads = do_piece.reshape(count, heads, HD)
    scores = jnp.einsum("qhd,khd->hqk", q_heads, kh, preferred_element_type=jnp.float32) * scale
    probs = jnp.where(
        allowed[None], jnp.exp(jnp.where(allowed[None], scores, NEG) - lse_all.T[:, :, None]), 0.0
    )
    dv_acc = jnp.einsum(
        "hqk,qhd->khd", probs.astype(jnp.bfloat16), do_heads, preferred_element_type=jnp.float32
    )
    d_probs = jnp.einsum("qhd,khd->hqk", do_heads, vh, preferred_element_type=jnp.float32)
    d_scores = (probs * (d_probs - delta_all.T[:, :, None])).astype(jnp.bfloat16)
    dk_acc = jnp.einsum("hqk,qhd->khd", d_scores, q_heads, preferred_element_type=jnp.float32)
    d_queries = (dq_sum * scale).astype(jnp.bfloat16).reshape(1, rows, width)
    d_keys = (dk_acc * scale).astype(jnp.bfloat16).reshape(1, rows, width)
    d_values = dv_acc.astype(jnp.bfloat16).reshape(1, rows, width)
    local_grad = lax.dot_general(
        attended, cot_full, (((0,), (0,)), ((), ())), preferred_element_type=jnp.float32
    )
    d_w_out = lax.psum_scatter(local_grad, ("dp", "blk"), scatter_dimension=1, tiled=True)
    return (mixed[None], d_queries, d_keys, d_values, d_w_out)


def solution(mesh):
    placed = (
        P("dp", "blk", "mp"),
        P("dp", "blk", "mp"),
        P("dp", "blk", "mp"),
        P("dp", "blk"),
        P("mp", None),
        P("dp", "blk", "mp"),
    )
    nd, nb, nm = mesh.shape["dp"], mesh.shape["blk"], mesh.shape["mp"]
    body = per_device
    if nb == 2 and nd == nm and nd % 2 == 0 and nd > 2:
        body = functools.partial(fused, nd, nm)
    return jax.shard_map(
        body,
        mesh=mesh,
        in_specs=placed,
        out_specs=(
            P("dp", "blk", "mp"),
            P("dp", "blk", "mp"),
            P("dp", "blk", "mp"),
            P("dp", "blk", "mp"),
            P("mp", ("dp", "blk")),
        ),
        check_vma=False,
    )
```

```python
import functools

import jax
import jax.numpy as jnp
from jax import lax
from jax.experimental import pallas as pl
from jax.experimental.pallas import tpu as pltpu
from jax.sharding import PartitionSpec as P

HD = 128
NEG = -1e30
MESH = pl.DeviceIdType.MESH
NN = (((1,), (0,)), ((), ()))
NT = (((1,), (1,)), ((), ()))
TN = (((0,), (0,)), ((), ()))


def dot(a, b, dims):
    return lax.dot_general(a, b, dims, preferred_element_type=jnp.float32)


def fused_kernel(
    nd, nm, chunks,
    q_hbm, k_hbm, v_hbm, clip_hbm, w_hbm, cot_hbm,
    mixed_hbm, dq_hbm, dk_hbm, dv_hbm, dw_hbm,
    mixed_ref, dq_ref, dk_ref, dv_ref, dw_ref, out_sem,
    q_ref, k_ref, v_ref, clip_ref, w_ref, cot_full, cot_cols, att_all, kv_prev, clip_send, clip_prev,
    p_own, p_prev, d_att, dkv_own, dkv_send, dkv_recv,
    up_out, up_in, down_out, down_in,
    in_sem, w_sem, own_sem, kv_ssem, kv_rsem, ag_up_ssem, ag_dn_ssem, ag_rsem,
    cc_ssem, cc_rsem, at_ssem, at_rsem,
    up_ssem, up_rsem, dn_ssem, dn_rsem, dkv_ssem, dkv_rsem,
):
    nb = 2
    d, b, m = lax.axis_index("dp"), lax.axis_index("blk"), lax.axis_index("mp")
    me = d * nb + b
    group = nd * nb
    rows, width = q_ref.shape[1], q_ref.shape[2]
    heads = width // HD
    scale = HD ** (-0.5)
    piece = cot_full.shape[2]
    half = piece // nb
    part = piece // chunks

    def remote(src, dst, ssem, rsem, device):
        return pltpu.make_async_remote_copy(
            src_ref=src, dst_ref=dst, send_sem=ssem, recv_sem=rsem,
            device_id=device, device_id_type=MESH,
        )

    w_copy = pltpu.make_async_copy(w_hbm, w_ref, w_sem)
    fetches = [
        pltpu.make_async_copy(src, dst, in_sem.at[i])
        for i, (src, dst) in enumerate((
            (cot_hbm.at[0], cot_full.at[m]), (k_hbm, k_ref), (v_hbm, v_ref), (q_hbm, q_ref),
            (clip_hbm, clip_ref),
        ))
    ]
    for copy in fetches:
        copy.start()
    w_copy.start()

    barrier = pltpu.get_barrier_semaphore()
    for off in range(1, group):
        other = lax.rem(me + off, group)
        pl.semaphore_signal(
            barrier, inc=1, device_id=(other // nb, lax.rem(other, nb), m), device_id_type=MESH
        )

    @pl.when(m > 0)
    def _():
        pl.semaphore_signal(barrier, inc=1, device_id=(d, b, m - 1), device_id_type=MESH)

    @pl.when(m < nm - 1)
    def _():
        pl.semaphore_signal(barrier, inc=1, device_id=(d, b, m + 1), device_id_type=MESH)

    clip_send[...] = jnp.zeros_like(clip_send)
    for copy in fetches:
        copy.wait()
    clip_send[0:1, 0:rows] = clip_ref[...]
    pl.semaphore_wait(
        barrier, group - 1 + jnp.where(m > 0, 1, 0) + jnp.where(m < nm - 1, 1, 0)
    )

    def kv_copies():
        peer = (d, 1, m)
        return (
            remote(k_ref.at[0], kv_prev.at[0], kv_ssem.at[0], kv_rsem.at[0], peer),
            remote(v_ref.at[0], kv_prev.at[1], kv_ssem.at[1], kv_rsem.at[1], peer),
            remote(clip_send, clip_prev, kv_ssem.at[2], kv_rsem.at[2], peer),
        )

    def gather_up(shard):
        return remote(
            cot_full.at[shard], cot_full.at[shard], ag_up_ssem.at[shard], ag_rsem.at[shard],
            (d, b, m + 1),
        )

    def gather_down(shard):
        return remote(
            cot_full.at[shard], cot_full.at[shard], ag_dn_ssem.at[shard], ag_rsem.at[shard],
            (d, b, m - 1),
        )

    def column_copy(shard, to_b):
        return remote(
            cot_full.at[shard, :, pl.ds(to_b * half, half)], cot_cols.at[me],
            cc_ssem.at[shard, to_b], cc_rsem.at[me], (shard, to_b, m),
        )

    def own_copy(to_b):
        return pltpu.make_async_copy(
            cot_full.at[d, :, pl.ds(to_b * half, half)], cot_cols.at[me], own_sem
        )

    def each_column(shard, away, here):
        for to_b in range(nb):
            is_me = jnp.logical_and(shard == d, b == to_b)

            @pl.when(jnp.logical_not(is_me))
            def _():
                away(column_copy(shard, to_b))

            @pl.when(is_me)
            def _():
                here(own_copy(to_b))

    def start(copy):
        copy.start()

    @pl.when(m < nm - 1)
    def _():
        gather_up(m).start()

    @pl.when(m > 0)
    def _():
        gather_down(m).start()

    @pl.when(b == 0)
    def _():
        for copy in kv_copies():
            copy.start()

    @pl.when(b == 1)
    def _():
        each_column(m, start, start)

    def gather_step(step):
        @pl.when(m - step >= 0)
        def _():
            shard = m - step
            gather_down(shard).wait_recv()

            @pl.when(m < nm - 1)
            def _():
                gather_up(shard).start()

            each_column(shard, start, start)

        @pl.when(m + step < nm)
        def _():
            shard = m + step
            gather_up(shard).wait_recv()

            @pl.when(m > 0)
            def _():
                gather_down(shard).start()

            each_column(shard, start, start)

    row = lax.broadcasted_iota(jnp.int32, (rows, rows), 0)
    col = lax.broadcasted_iota(jnp.int32, (rows, rows), 1)

    def clip_rows(ref):
        return jnp.broadcast_to(ref[0:1, 0:rows], (rows, rows))

    def own_scores(h):
        cols = pl.ds(h * HD, HD)
        return jnp.where(seen, dot(q_ref[0, :, cols], k_ref[0, :, cols], NT) * scale, NEG)

    here = clip_rows(clip_send)
    mine = jnp.sum(jnp.where(row == col, here, 0), axis=1, keepdims=True)
    seen = jnp.logical_and(col <= row, here == mine)

    @pl.when(b == 0)
    def _():
        for h in range(heads):
            cols = pl.ds(h * HD, HD)
            s = own_scores(h)
            e = jnp.exp(s - jnp.max(s, axis=1, keepdims=True))
            e = e * (1.0 / jnp.sum(e, axis=1, keepdims=True))
            p_own[h] = e
            att = dot(e.astype(jnp.bfloat16), v_ref[0, :, cols], NN)
            att_all[me, :, cols] = att.astype(jnp.bfloat16)

    @pl.when(b == 1)
    def _():
        for h in range(heads):
            p_own[h] = own_scores(h)

    gather_step(1)

    @pl.when(b == 0)
    def _():
        each_column(m, start, start)

    @pl.when(b == 1)
    def _():
        k_copy, v_copy, clip_copy = kv_copies()
        clip_copy.wait_recv()
        k_copy.wait_recv()
        earlier = clip_rows(clip_prev) == mine
        for h in range(heads):
            cols = pl.ds(h * HD, HD)
            s = p_own[h]
            t = jnp.where(
                earlier, dot(q_ref[0, :, cols], kv_prev[0, :, cols], NT) * scale, NEG
            )
            peak = jnp.maximum(
                jnp.max(s, axis=1, keepdims=True), jnp.max(t, axis=1, keepdims=True)
            )
            e, f = jnp.exp(s - peak), jnp.exp(t - peak)
            inverse = 1.0 / (
                jnp.sum(e, axis=1, keepdims=True) + jnp.sum(f, axis=1, keepdims=True)
            )
            e, f = e * inverse, f * inverse
            p_own[h] = e
            p_prev[h] = f
            dkv_own[0, :, cols] = dot(e.astype(jnp.bfloat16), v_ref[0, :, cols], NN)
        v_copy.wait_recv()
        for h in range(heads):
            cols = pl.ds(h * HD, HD)
            att = dkv_own[0, :, cols] + dot(
                p_prev[h].astype(jnp.bfloat16), kv_prev[1, :, cols], NN
            )
            att_all[me, :, cols] = att.astype(jnp.bfloat16)

    pairs = group // 2
    core = lax.rem(d, 2)
    partner = (d + 1 - 2 * core, b, m)
    pair = (d // 2) * nb + b

    def att_slot(off):
        other = lax.rem(pair + off, pairs)
        return (other // nb) * 2 + core, lax.rem(other, nb)

    def att_copy(off):
        to_d, to_b = att_slot(off)
        return remote(
            att_all.at[me], att_all.at[me], at_ssem.at[off], at_rsem.at[me], (to_d, to_b, m)
        )

    def att_pass(off):
        of_d, of_b = att_slot(off)
        slot = of_d * nb + of_b
        return remote(
            att_all.at[slot], att_all.at[slot], at_ssem.at[pairs + off], at_rsem.at[slot], partner
        )

    for off in range(1, pairs):
        att_copy(off).start()
    att_pass(0).start()

    w_copy.wait()

    def partial(dest, c):
        at = pl.multiple_of(dest * piece + c * part, part)
        return dot(att_all[me], w_ref[:, pl.ds(at, part)], NN)

    def sum_up(dest, c):
        return remote(
            up_out.at[dest, c], up_in.at[dest, c], up_ssem.at[dest, c], up_rsem.at[dest, c],
            (d, b, m + 1),
        )

    def sum_down(dest, c):
        return remote(
            down_out.at[dest, c], down_in.at[dest, c], dn_ssem.at[dest, c], dn_rsem.at[dest, c],
            (d, b, m - 1),
        )

    def chain_step(step):
        for c in range(chunks):
            @pl.when(step >= m)
            def _():
                dest = nm - 1 - step + m
                mine = partial(dest, c)

                @pl.when(m == 0)
                def _():
                    up_out[dest, c] = mine.astype(jnp.bfloat16)

                @pl.when(m > 0)
                def _():
                    sum_up(dest, c).wait_recv()
                    up_out[dest, c] = (
                        mine + up_in[dest, c].astype(jnp.float32)
                    ).astype(jnp.bfloat16)

                sum_up(dest, c).start()

            @pl.when(step >= nm - 1 - m)
            def _():
                dest = step - (nm - 1 - m)
                mine = partial(dest, c)

                @pl.when(m == nm - 1)
                def _():
                    down_out[dest, c] = mine.astype(jnp.bfloat16)

                @pl.when(m < nm - 1)
                def _():
                    sum_down(dest, c).wait_recv()
                    down_out[dest, c] = (
                        mine + down_in[dest, c].astype(jnp.float32)
                    ).astype(jnp.bfloat16)

                sum_down(dest, c).start()

    at_end = jnp.logical_or(m == 0, m == nm - 1)
    for step in range(nm - 2):
        chain_step(step)
        if step == nm - 3:
            @pl.when(at_end)
            def _():
                chain_step(nm - 2)

        gather_step(step + 2)

    total = dot(cot_full[0], w_ref[:, 0:piece], NT)
    for shard in range(1, nm):
        total = total + dot(cot_full[shard], w_ref[:, shard * piece:(shard + 1) * piece], NT)
    d_att[...] = total.astype(jnp.bfloat16)

    def dkv_copy():
        return remote(dkv_send, dkv_recv, dkv_ssem, dkv_rsem, (d, 0, m))

    def backward(use_prev):
        for h in range(heads):
            cols = pl.ds(h * HD, HD)
            do = d_att[:, cols]
            q = q_ref[0, :, cols]
            delta = jnp.sum(
                do.astype(jnp.float32) * att_all[me, :, cols].astype(jnp.float32),
                axis=1, keepdims=True,
            )
            e = p_own[h]
            ds = (e * (dot(do, v_ref[0, :, cols], NT) - delta)).astype(jnp.bfloat16)
            dq = dot(ds, k_ref[0, :, cols], NN)
            dk = dot(ds, q, TN) * scale
            dv = dot(e.astype(jnp.bfloat16), do, TN)
            if use_prev:
                f = p_prev[h]
                dt = (f * (dot(do, kv_prev[1, :, cols], NT) - delta)).astype(jnp.bfloat16)
                dq = dq + dot(dt, kv_prev[0, :, cols], NN)
                dkv_send[0, :, cols] = (dot(dt, q, TN) * scale).astype(jnp.bfloat16)
                dkv_send[1, :, cols] = dot(f.astype(jnp.bfloat16), do, TN).astype(jnp.bfloat16)
                dk_ref[0, :, cols] = dk.astype(jnp.bfloat16)
                dv_ref[0, :, cols] = dv.astype(jnp.bfloat16)
            else:
                dkv_own[0, :, cols] = dk
                dkv_own[1, :, cols] = dv
            dq_ref[0, :, cols] = (dq * scale).astype(jnp.bfloat16)

    @pl.when(b == 0)
    def _():
        backward(False)

    @pl.when(b == 1)
    def _():
        backward(True)
        dkv_copy().start()

    stores = [
        pltpu.make_async_copy(src, dst, out_sem.at[i])
        for i, (src, dst) in enumerate((
            (mixed_ref, mixed_hbm), (dq_ref, dq_hbm), (dk_ref, dk_hbm), (dv_ref, dv_hbm),
            (dw_ref, dw_hbm),
        ))
    ]
    stores[1].start()

    for off in range(1, pairs):
        att_pass(off).wait_recv()
        att_pass(off).start()

    @pl.when(jnp.logical_not(at_end))
    def _():
        chain_step(nm - 2)

    def arrived(buffer, slot, sems):
        remote(
            buffer.at[slot], buffer.at[slot], at_ssem.at[0], sems.at[slot], partner
        ).wait_recv()

    for off in range(nd):
        first = lax.rem(d + off, nd) * nb
        if off == 0:
            own_copy(0).wait()
            arrived(cot_cols, first + 1 - b, cc_rsem)
        else:
            for to_b in range(nb):
                arrived(cot_cols, first + to_b, cc_rsem)
        if off % 2 == 1:
            for to_b in range(nb):
                arrived(att_all, first + to_b, at_rsem)
        grad = dot(
            att_all[pl.ds(first, nb)].reshape(nb * rows, width),
            cot_cols[pl.ds(first, nb)].reshape(nb * rows, half), TN,
        )
        dw_ref[...] = grad if off == 0 else dw_ref[...] + grad

    stores[4].start()

    @pl.when(b == 0)
    def _():
        dkv_copy().wait_recv()
        dk_ref[0] = (dkv_own[0] + dkv_recv[0].astype(jnp.float32)).astype(jnp.bfloat16)
        dv_ref[0] = (dkv_own[1] + dkv_recv[1].astype(jnp.float32)).astype(jnp.bfloat16)

    stores[2].start()
    stores[3].start()

    for c in range(chunks):
        mine = partial(m, c)
        at = slice(c * part, (c + 1) * part)

        @pl.when(m > 0)
        def _():
            sum_up(m, c).wait_recv()

        @pl.when(m < nm - 1)
        def _():
            sum_down(m, c).wait_recv()

        @pl.when(m == 0)
        def _():
            mixed_ref[0, :, at] = (mine + down_in[m, c].astype(jnp.float32)).astype(jnp.bfloat16)

        @pl.when(m == nm - 1)
        def _():
            mixed_ref[0, :, at] = (mine + up_in[m, c].astype(jnp.float32)).astype(jnp.bfloat16)

        @pl.when(jnp.logical_and(m > 0, m < nm - 1))
        def _():
            mixed_ref[0, :, at] = (
                mine + up_in[m, c].astype(jnp.float32) + down_in[m, c].astype(jnp.float32)
            ).astype(jnp.bfloat16)

    stores[0].start()

    for shard in range(nm):
        @pl.when(jnp.logical_and(m < nm - 1, shard <= m))
        def _():
            gather_up(shard).wait_send()

        @pl.when(jnp.logical_and(m > 0, shard >= m))
        def _():
            gather_down(shard).wait_send()

        for to_b in range(nb):
            @pl.when(jnp.logical_not(jnp.logical_and(shard == d, b == to_b)))
            def _():
                column_copy(shard, to_b).wait_send()

        for c in range(chunks):
            @pl.when(shard > m)
            def _():
                sum_up(shard, c).wait_send()

            @pl.when(shard < m)
            def _():
                sum_down(shard, c).wait_send()

    for off in range(1, pairs):
        att_copy(off).wait_send()
    for off in range(pairs):
        att_pass(off).wait_send()

    @pl.when(b == 0)
    def _():
        for copy in kv_copies():
            copy.wait_send()

    @pl.when(b == 1)
    def _():
        dkv_copy().wait_send()

    for copy in stores:
        copy.wait()


def write_kernel(*refs):
    sources, results, held = refs[:5], refs[5:10], refs[10:15]
    in_sem, out_sem = refs[15:]
    reads = [pltpu.make_async_copy(sources[i], held[i], in_sem.at[i]) for i in range(5)]
    writes = [pltpu.make_async_copy(held[i], results[i], out_sem.at[i]) for i in range(5)]
    reads, writes = reads[::-1], writes[::-1]
    for copy in reads:
        copy.start()
    for read, write in zip(reads, writes):
        read.wait()
        write.start()
    for copy in writes:
        copy.wait()


def fused(nd, nm, queries, keys, values, clip_ids, w_out, cotangent):
    nb, chunks = 2, 2
    group = nd * nb
    _, rows, width = queries.shape
    piece = cotangent.shape[2]
    half, part = piece // nb, piece // chunks
    heads = width // HD
    lanes = -(-rows // 128) * 128
    bf16, f32 = jnp.bfloat16, jnp.float32
    dma = pltpu.SemaphoreType.DMA
    results = pl.pallas_call(
        functools.partial(fused_kernel, nd, nm, chunks),
        out_shape=(
            jax.ShapeDtypeStruct((1, rows, piece), bf16),
            jax.ShapeDtypeStruct((1, rows, width), bf16),
            jax.ShapeDtypeStruct((1, rows, width), bf16),
            jax.ShapeDtypeStruct((1, rows, width), bf16),
            jax.ShapeDtypeStruct((width, half), f32),
        ),
        in_specs=[pl.BlockSpec(memory_space=pltpu.HBM)] * 6,
        out_specs=(pl.BlockSpec(memory_space=pltpu.HBM),) * 5,
        scratch_shapes=[
            pltpu.VMEM((1, rows, piece), bf16),
            pltpu.VMEM((1, rows, width), bf16),
            pltpu.VMEM((1, rows, width), bf16),
            pltpu.VMEM((1, rows, width), bf16),
            pltpu.VMEM((width, half), f32),
            dma((5,)),
            pltpu.VMEM(queries.shape, bf16),
            pltpu.VMEM(queries.shape, bf16),
            pltpu.VMEM(queries.shape, bf16),
            pltpu.VMEM(clip_ids.shape, jnp.int32),
            pltpu.VMEM(w_out.shape, bf16),
            pltpu.VMEM((nm, rows, piece), bf16),
            pltpu.VMEM((group, rows, half), bf16),
            pltpu.VMEM((group, rows, width), bf16),
            pltpu.VMEM((2, rows, width), bf16),
            pltpu.VMEM((8, lanes), jnp.int32),
            pltpu.VMEM((8, lanes), jnp.int32),
            pltpu.VMEM((heads, rows, rows), f32),
            pltpu.VMEM((heads, rows, rows), f32),
            pltpu.VMEM((rows, width), bf16),
            pltpu.VMEM((2, rows, width), f32),
            pltpu.VMEM((2, rows, width), bf16),
            pltpu.VMEM((2, rows, width), bf16),
            pltpu.VMEM((nm, chunks, rows, part), bf16),
            pltpu.VMEM((nm, chunks, rows, part), bf16),
            pltpu.VMEM((nm, chunks, rows, part), bf16),
            pltpu.VMEM((nm, chunks, rows, part), bf16),
            dma((5,)), dma, dma, dma((3,)), dma((3,)), dma((nm,)), dma((nm,)), dma((nm,)),
            dma((nm, nb)), dma((group,)), dma((group,)), dma((group,)),
            dma((nm, chunks)), dma((nm, chunks)), dma((nm, chunks)), dma((nm, chunks)), dma, dma,
        ],
        compiler_params=pltpu.CompilerParams(
            collective_id=0, has_side_effects=True, vmem_limit_bytes=61 * 1024 * 1024
        ),
    )(queries, keys, values, clip_ids, w_out, cotangent)
    return pl.pallas_call(
        write_kernel,
        out_shape=tuple(jax.ShapeDtypeStruct(x.shape, x.dtype) for x in results),
        in_specs=[pl.BlockSpec(memory_space=pltpu.HBM)] * 5,
        out_specs=(pl.BlockSpec(memory_space=pltpu.HBM),) * 5,
        scratch_shapes=[pltpu.VMEM(x.shape, x.dtype) for x in results] + [dma((5,)), dma((5,))],
        compiler_params=pltpu.CompilerParams(vmem_limit_bytes=61 * 1024 * 1024),
    )(*results)


def seen_mask(q_pos, q_clip, k_pos, k_clip):
    return (k_pos[None, :] <= q_pos[:, None]) & (k_clip[None, :] == q_clip[:, None])


def per_device(queries, keys, values, clip_ids, w_out, cotangent):
    q_here = queries[0]
    k_here = keys[0]
    v_here = values[0]
    rows = q_here.shape[0]
    width = q_here.shape[1]
    heads = width // HD
    scale = HD ** (-0.5)
    first = lax.axis_index("blk") * rows
    q_pos = first + jnp.arange(rows, dtype=jnp.int32)
    clips_all = lax.all_gather(clip_ids[0], "blk", axis=0, tiled=True)
    clip_here = lax.dynamic_slice_in_dim(clips_all, first, rows, 0)
    qh = q_here.reshape(rows, heads, HD)
    kh = k_here.reshape(rows, heads, HD)
    vh = v_here.reshape(rows, heads, HD)
    k_piece = lax.all_gather(k_here, "blk", axis=0, tiled=True)
    v_piece = lax.all_gather(v_here, "blk", axis=0, tiled=True)
    count = k_piece.shape[0]
    k_pos = jnp.arange(count, dtype=jnp.int32)
    k_clip = clips_all
    allowed = seen_mask(q_pos, clip_here, k_pos, k_clip)
    peak = jnp.full((heads, rows), NEG, jnp.float32)
    accum = jnp.zeros((rows, heads, HD), jnp.float32)
    scores = (
        jnp.einsum(
            "qhd,khd->hqk",
            qh,
            k_piece.reshape(count, heads, HD),
            preferred_element_type=jnp.float32,
        )
        * scale
    )
    scores = jnp.where(allowed[None], scores, NEG)
    new_peak = jnp.maximum(peak, jnp.max(scores, axis=-1))
    factor = jnp.exp(peak - new_peak)
    probs = jnp.where(allowed[None], jnp.exp(scores - new_peak[:, :, None]), 0.0)
    total = jnp.sum(probs, axis=-1)
    v_block = v_piece.reshape(count, heads, HD).astype(jnp.float32)
    accum = accum * factor.T[:, :, None] + jnp.einsum(
        "hqk,khd->qhd",
        probs,
        v_block,
        precision=lax.Precision.HIGHEST,
        preferred_element_type=jnp.float32,
    )
    peak, total, accum = (new_peak, total, accum)
    lse = peak + jnp.log(total)
    attended = (accum / total.T[:, :, None]).astype(jnp.bfloat16).reshape(rows, width)
    partial_value = jnp.dot(attended, w_out, preferred_element_type=jnp.float32)
    mixed = lax.psum_scatter(partial_value, "mp", scatter_dimension=1, tiled=True).astype(
        jnp.bfloat16
    )
    cot_full = lax.all_gather(cotangent[0], "mp", axis=1, tiled=True)
    d_att = lax.dot_general(
        cot_full, w_out, (((1,), (1,)), ((), ())), preferred_element_type=jnp.float32
    ).astype(jnp.bfloat16)
    doh = d_att.reshape(rows, heads, HD)
    delta = jnp.sum(
        doh.astype(jnp.float32) * attended.reshape(rows, heads, HD).astype(jnp.float32), axis=-1
    )
    lse_all, delta_all = (
        lax.all_gather(lse.T, "blk", axis=0, tiled=True),
        lax.all_gather(delta, "blk", axis=0, tiled=True),
    )
    k_piece = lax.all_gather(k_here, "blk", axis=0, tiled=True)
    v_piece = lax.all_gather(v_here, "blk", axis=0, tiled=True)
    count = k_piece.shape[0]
    k_pos = jnp.arange(count, dtype=jnp.int32)
    k_clip = clips_all
    allowed = seen_mask(q_pos, clip_here, k_pos, k_clip)
    k_heads = k_piece.reshape(count, heads, HD)
    scores = jnp.einsum("qhd,khd->hqk", qh, k_heads, preferred_element_type=jnp.float32) * scale
    probs = jnp.where(
        allowed[None], jnp.exp(jnp.where(allowed[None], scores, NEG) - lse[:, :, None]), 0.0
    )
    d_probs = jnp.einsum(
        "qhd,khd->hqk", doh, v_piece.reshape(count, heads, HD), preferred_element_type=jnp.float32
    )
    d_scores = (probs * (d_probs - delta.T[:, :, None])).astype(jnp.bfloat16)
    dq_sum = jnp.einsum("hqk,khd->qhd", d_scores, k_heads, preferred_element_type=jnp.float32)
    q_piece = lax.all_gather(q_here, "blk", axis=0, tiled=True)
    do_piece = lax.all_gather(d_att, "blk", axis=0, tiled=True)
    count = q_piece.shape[0]
    p_pos = jnp.arange(count, dtype=jnp.int32)
    allowed = seen_mask(p_pos, clips_all, q_pos, clip_here)
    q_heads = q_piece.reshape(count, heads, HD)
    do_heads = do_piece.reshape(count, heads, HD)
    scores = jnp.einsum("qhd,khd->hqk", q_heads, kh, preferred_element_type=jnp.float32) * scale
    probs = jnp.where(
        allowed[None], jnp.exp(jnp.where(allowed[None], scores, NEG) - lse_all.T[:, :, None]), 0.0
    )
    dv_acc = jnp.einsum(
        "hqk,qhd->khd", probs.astype(jnp.bfloat16), do_heads, preferred_element_type=jnp.float32
    )
    d_probs = jnp.einsum("qhd,khd->hqk", do_heads, vh, preferred_element_type=jnp.float32)
    d_scores = (probs * (d_probs - delta_all.T[:, :, None])).astype(jnp.bfloat16)
    dk_acc = jnp.einsum("hqk,qhd->khd", d_scores, q_heads, preferred_element_type=jnp.float32)
    d_queries = (dq_sum * scale).astype(jnp.bfloat16).reshape(1, rows, width)
    d_keys = (dk_acc * scale).astype(jnp.bfloat16).reshape(1, rows, width)
    d_values = dv_acc.astype(jnp.bfloat16).reshape(1, rows, width)
    local_grad = lax.dot_general(
        attended, cot_full, (((0,), (0,)), ((), ())), preferred_element_type=jnp.float32
    )
    d_w_out = lax.psum_scatter(local_grad, ("dp", "blk"), scatter_dimension=1, tiled=True)
    return (mixed[None], d_queries, d_keys, d_values, d_w_out)


def solution(mesh):
    placed = (
        P("dp", "blk", "mp"),
        P("dp", "blk", "mp"),
        P("dp", "blk", "mp"),
        P("dp", "blk"),
        P("mp", None),
        P("dp", "blk", "mp"),
    )
    nd, nb, nm = mesh.shape["dp"], mesh.shape["blk"], mesh.shape["mp"]
    body = per_device
    if nb == 2 and nd == nm and nd % 2 == 0 and nd > 2:
        body = functools.partial(fused, nd, nm)
    return jax.shard_map(
        body,
        mesh=mesh,
        in_specs=placed,
        out_specs=(
            P("dp", "blk", "mp"),
            P("dp", "blk", "mp"),
            P("dp", "blk", "mp"),
            P("dp", "blk", "mp"),
            P("mp", ("dp", "blk")),
        ),
        check_vma=False,
    )
```
